512 devices in a mesh: ctx: 16 (over z_lo, core), head: 32 (over z_hi, y, x).
Axes of the slice: x: 4, y: 4, z: 16 (z_hi: 2, z_lo: 8; z = z_hi * 8 + z_lo), core: 2. Of those that a mesh axis runs over, the one named last changes fastest.
Arguments:
- queries: bfloat16 [4096, 8192], P('ctx', 'head'), may hold values from -5 to 5
- key_rows: bfloat16 [4096, 1024], P('ctx'), may hold values from -5 to 5
- value_rows: bfloat16 [4096, 1024], P('ctx'), may hold values from -6 to 6
- state_input: bfloat16 [4096, 8192], P('ctx', 'head'), may hold values from -6 to 6
- state_write: bfloat16 [4096, 8192], P('ctx', 'head'), may hold values from -0.119628906 to 0.119628906
- state_read: bfloat16 [4096, 8192], P('ctx', 'head'), may hold values from -6 to 6
- gate_input: bfloat16 [4096, 8192], P('ctx', 'head'), may hold values from -6 to 6
- decay_codes: int32 [4096, 64], P('ctx', 'head'), may hold values from 1 to 8192
- decay_rates: float32 [64], P('head'), may hold values from 2.9296875e-05 to 0.03
- skip_gain: float32 [64], P('head'), may hold values from 0.5 to 2
- norm_gain: float32 [8192], P('head'), may hold values from 0.5 to 1.5
- attend_readout: float32 [8192], P('head'), may hold values from -1.5 to 1.5
- state_readout: float32 [8192], P('head'), may hold values from -0.12 to 0.12
- segment_index: int32 [4096], P('ctx'), may hold values from 0 to 31, never falling along the last dimension, each value on 1 to 256 neighbouring positions
Outputs:
- attended: bfloat16 [4096, 8192], P('ctx', 'head')
- state_mixed: bfloat16 [4096, 8192], P('ctx', 'head')
- segment_values: float32 [32], replicated
The draws below stay inside these ranges and needn't reach their ends.
All inputs are finite; a program needn't handle non-finite values.
Results may differ from the reference program's by a relative error of at most 0.018.
Values may be sent and summed in bfloat16 or wider, within the bound.
No kernel may reach another device: no remote copies, remote signals or barrier semaphores. Data moves between devices by JAX's collectives and lax.ppermute only.
A program may use at most 64 MiB of HBM per device.

```python
import math
import jax
import jax.numpy as jnp
import numpy as np
from jax import lax

HEADS = 64
KV_HEADS = 8
HEAD_DIM = 128
SCAN_HEADS = 64
SCAN_DIM = 128
STATE = 128
BLOCK = 128
SPIKE_SLOTS = 2
SEQUENCE_SLOTS = 4096
SEGMENTS = 32
SEG_MOST = 256
SPIKE_DECAY_RATE = 8192


def plant_pair(key):
    query_key = jax.random.fold_in(key, 11)
    other_key = jax.random.fold_in(key, 12)
    width = HEADS * HEAD_DIM
    narrow = KV_HEADS * HEAD_DIM
    query_draw = jnp.clip(jax.random.normal(query_key, (SEQUENCE_SLOTS, width), jnp.float32), -5.0, 5.0)
    keyset = jnp.clip(jax.random.normal(other_key, (SEQUENCE_SLOTS, narrow), jnp.float32), -5.0, 5.0)
    return (query_draw, keyset)


def draw_queries(key, part):
    return plant_pair(key)[0].astype(jnp.bfloat16)


def draw_key_rows(key, part):
    return plant_pair(key)[1].astype(jnp.bfloat16)


def draw_decay_rates(key, part):
    share = 0.5
    quick_flag = jax.random.bernoulli(jax.random.fold_in(key, 21), share, (SCAN_HEADS,))
    quick = jnp.exp(jax.random.uniform(jax.random.fold_in(key, 22), (SCAN_HEADS,), jnp.float32, math.log(0.015), math.log(0.03)))
    slow = jnp.exp(jax.random.uniform(jax.random.fold_in(key, 23), (SCAN_HEADS,), jnp.float32, math.log(0.3), math.log(0.8))) / (2.5 * SEQUENCE_SLOTS)
    return jnp.where(quick_flag, quick, slow).astype(jnp.float32)


def draw_decay_codes(key, part):
    starting_shift = jax.random.randint(jax.random.fold_in(key, 31), (SEQUENCE_SLOTS, SCAN_HEADS), 1, 5, dtype=jnp.int32)
    flagged_slots = jax.random.randint(jax.random.fold_in(key, 32), (SPIKE_SLOTS,), 0, SEQUENCE_SLOTS, dtype=jnp.int32)
    places = jnp.arange(SEQUENCE_SLOTS, dtype=jnp.int32)
    removed_slots = jnp.any(places[:, None] == flagged_slots[None, :], axis=1)
    return jnp.where(removed_slots[:, None], SPIKE_DECAY_RATE, starting_shift).astype(jnp.int32)


def shard_levels(stream_key, extent, cuts, smallest, top_value):
    factor_of = 1.0
    for dim, shards_of in cuts:
        steps = jax.random.uniform(jax.random.fold_in(jax.random.fold_in(stream_key, 6), dim), (shards_of,), jnp.float32, smallest / len(cuts), top_value / len(cuts))
        factor_of = factor_of * jnp.repeat(jnp.exp(steps), extent[dim] // shards_of).reshape((-1,) + (1,) * (len(extent) - 1 - dim))
    return factor_of


def split_up(count, total, limit, lean):
    loads = [(1 << 20) // math.isqrt(rank ** lean) + 1 for rank in range(2, count + 1)]
    surplus, given = total - limit - (count - 1), [1] * (count - 1)
    while surplus > 0:
        movable = [i for i in range(count - 1) if given[i] < limit]
        whole, left = sum([loads[i] for i in movable]), surplus
        for i in movable:
            addition = min(limit - given[i], max(1, left * loads[i] // whole), surplus)
            given[i] = given[i] + addition
            surplus = surplus - addition
    return np.array([limit] + given)


def ragged(own_key, number_of, total, most, slope):
    if number_of == 2:
        one = jax.random.randint(own_key, (), max(1, total - most), min(most, total - 1) + 1)
        return jnp.stack([one, total - one])
    tallies = jnp.asarray(split_up(number_of, total, most, slope), jnp.int32)
    pairs = (number_of - 1) // 2
    giver, taker = tallies[1:1 + 2 * pairs:2], tallies[2:2 + 2 * pairs:2]
    slack = jnp.minimum(giver - 1, most - taker)
    shifted = jax.random.randint(jax.random.fold_in(own_key, 1), (pairs,), 0, 1 << 20) % (slack + 1)
    tallies = tallies.at[1:1 + 2 * pairs:2].set(giver - shifted).at[2:2 + 2 * pairs:2].set(taker + shifted)
    return tallies[jax.random.permutation(jax.random.fold_in(own_key, 2), number_of)]


def scatter_about(rng, dims, deviation, most, shards=(), kind=jnp.bfloat16):
    array = jax.random.normal(rng, dims, jnp.float32) * deviation
    if len(shards) > 0:
        array = shard_levels(rng, dims, shards, -0.22, 0.18) * array
    return jnp.clip(array, min=-most, max=most).astype(kind)


def setup_inputs(seed: int = 0) -> dict:
    arg_keys = jax.random.split(jax.random.key(seed), 15)
    queries = draw_queries(jax.random.fold_in(arg_keys[14], 71), 0)
    key_rows = draw_key_rows(jax.random.fold_in(arg_keys[14], 71), 0)
    value_rows = scatter_about(arg_keys[2], (SEQUENCE_SLOTS, KV_HEADS * HEAD_DIM), 1.0, 6.0, ((0, 16),))
    state_input = scatter_about(arg_keys[3], (SEQUENCE_SLOTS, SCAN_HEADS * SCAN_DIM), 1.0, 6.0, ((0, 16), (1, 32)))
    state_write = scatter_about(arg_keys[4], (SEQUENCE_SLOTS, SCAN_HEADS * STATE), 0.02, 0.119628906, ((0, 16), (1, 32)))
    state_read = scatter_about(arg_keys[5], (SEQUENCE_SLOTS, SCAN_HEADS * STATE), 1.0, 6.0, ((0, 16), (1, 32)))
    gate_input = scatter_about(arg_keys[6], (SEQUENCE_SLOTS, SCAN_HEADS * SCAN_DIM), 1.0, 6.0, ((0, 16), (1, 32)))
    decay_codes = draw_decay_codes(jax.random.fold_in(arg_keys[14], 71), 0)
    decay_rates = draw_decay_rates(jax.random.fold_in(arg_keys[14], 71), 0)
    skip_gain = jnp.clip(jnp.exp(math.log(2.0) - 1.3862944 * jax.random.uniform(arg_keys[9], (SCAN_HEADS,), jnp.float32) ** shard_levels(arg_keys[9], (SCAN_HEADS,), ((0, 32),), -0.2, 0.2)), 0.5, 2.0)
    norm_gain = jnp.clip(1.0 + 0.1 * jax.random.normal(arg_keys[10], (SCAN_HEADS * SCAN_DIM,), jnp.float32), 0.5, 1.5)
    attend_readout = scatter_about(arg_keys[11], (HEADS * HEAD_DIM,), 0.25, 1.5, ((0, 32),), jnp.float32)
    state_readout = scatter_about(arg_keys[12], (SCAN_HEADS * SCAN_DIM,), 0.02, 0.12, ((0, 32),), jnp.float32)
    segment_index = jnp.searchsorted(jnp.cumsum(ragged(arg_keys[13], SEGMENTS, SEQUENCE_SLOTS, SEG_MOST, 1)), jnp.arange(SEQUENCE_SLOTS), side="right").astype(jnp.int32)
    return {"queries": queries, "key_rows": key_rows, "value_rows": value_rows, "state_input": state_input, "state_write": state_write, "state_read": state_read, "gate_input": gate_input, "decay_codes": decay_codes, "decay_rates": decay_rates, "skip_gain": skip_gain, "norm_gain": norm_gain, "attend_readout": attend_readout, "state_readout": state_readout, "segment_index": segment_index}


def attend_head(query_head, key_head, value_head):
    rows = math.gcd(SEQUENCE_SLOTS, 512)
    scale = HEAD_DIM ** (-0.5)
    key_pos = jnp.arange(SEQUENCE_SLOTS, dtype=jnp.int32)

    def one_block(start):
        block = lax.dynamic_slice_in_dim(query_head, start, rows, 0)
        scores = jnp.dot(block, key_head.T, preferred_element_type=jnp.float32) * scale
        query_pos = start + jnp.arange(rows, dtype=jnp.int32)
        allowed = key_pos[None, :] <= query_pos[:, None]
        scores = jnp.where(allowed, scores, -jnp.inf)
        top = lax.optimization_barrier(jnp.max(scores, axis=1, keepdims=True))
        weights = jnp.exp(scores - top)
        total = lax.optimization_barrier(jnp.sum(weights, axis=1, keepdims=True))
        return jnp.dot(weights.astype(jnp.bfloat16), value_head, preferred_element_type=jnp.float32) / total
    starts = jnp.arange(SEQUENCE_SLOTS // rows, dtype=jnp.int32) * rows
    return lax.map(one_block, starts).reshape(SEQUENCE_SLOTS, HEAD_DIM)

def scan_head(inputs, write, read, logs, skip):
    blocks = SEQUENCE_SLOTS // BLOCK
    inputs_b = inputs.reshape(blocks, BLOCK, SCAN_DIM).astype(jnp.float32)
    write_b = write.reshape(blocks, BLOCK, STATE).astype(jnp.float32)
    read_b = read.reshape(blocks, BLOCK, STATE).astype(jnp.float32)
    run = jnp.cumsum(logs.reshape(blocks, BLOCK), axis=1)
    gap = run[:, :, None] - run[:, None, :]
    places = jnp.arange(BLOCK, dtype=jnp.int32)
    lower = places[:, None] >= places[None, :]
    decay = jnp.where(lower[None], jnp.exp(jnp.minimum(gap, 0.0)), 0.0)
    scores = jnp.einsum('btn,bsn->bts', read_b, write_b)
    mix = (scores * decay).astype(jnp.bfloat16)
    local = jnp.einsum('bts,bsp->btp', mix.astype(jnp.float32), inputs_b)
    tail = jnp.exp(run[:, -1:] - run)
    written = (write_b * tail[:, :, None]).astype(jnp.bfloat16)
    block_state = jnp.einsum('bsn,bsp->bnp', written.astype(jnp.float32), inputs_b)
    fade = jnp.exp(run[:, -1])

    def carry_step(state, item):
        fade_now, new_state = item
        return (fade_now * state + new_state, state)
    _, entering = lax.scan(carry_step, jnp.zeros((STATE, SCAN_DIM), jnp.float32), (fade, block_state))
    carried = jnp.exp(run)[:, :, None] * jnp.einsum('btn,bnp->btp', read_b, entering, precision=lax.Precision.HIGHEST)
    return (local + carried + skip * inputs_b).reshape(SEQUENCE_SLOTS, SCAN_DIM)

def reference(queries, key_rows, value_rows, state_input, state_write, state_read, gate_input, decay_codes, decay_rates, skip_gain, norm_gain, attend_readout, state_readout, segment_index):
    group = HEADS // KV_HEADS
    query_heads = jnp.transpose(queries.reshape(SEQUENCE_SLOTS, HEADS, HEAD_DIM), (1, 0, 2))
    key_heads = jnp.transpose(key_rows.reshape(SEQUENCE_SLOTS, KV_HEADS, HEAD_DIM), (1, 0, 2))
    value_heads = jnp.transpose(value_rows.reshape(SEQUENCE_SLOTS, KV_HEADS, HEAD_DIM), (1, 0, 2))

    def one_head(index):
        shared = index // group
        return attend_head(query_heads[index], key_heads[shared], value_heads[shared])
    outputs = lax.map(one_head, jnp.arange(HEADS, dtype=jnp.int32))
    attended = jnp.transpose(outputs, (1, 0, 2)).reshape(SEQUENCE_SLOTS, HEADS * HEAD_DIM).astype(jnp.bfloat16)
    log_decay = -decay_rates[None, :] * decay_codes.astype(jnp.float32)
    input_heads = jnp.transpose(state_input.reshape(SEQUENCE_SLOTS, SCAN_HEADS, SCAN_DIM), (1, 0, 2))
    write_heads = jnp.transpose(state_write.reshape(SEQUENCE_SLOTS, SCAN_HEADS, STATE), (1, 0, 2))
    read_heads = jnp.transpose(state_read.reshape(SEQUENCE_SLOTS, SCAN_HEADS, STATE), (1, 0, 2))
    mixed = lax.map(lambda item: scan_head(item[0], item[1], item[2], item[3], item[4]), (input_heads, write_heads, read_heads, log_decay.T, skip_gain))
    mixed_y = jnp.transpose(mixed, (1, 0, 2)).reshape(SEQUENCE_SLOTS, SCAN_HEADS * SCAN_DIM)
    gated = mixed_y * jax.nn.silu(gate_input.astype(jnp.float32))
    state_mixed = (gated * lax.rsqrt(lax.optimization_barrier(jnp.mean(gated * gated, axis=1, keepdims=True)) + 1e-05) * norm_gain[None, :]).astype(jnp.bfloat16)
    score = jnp.dot(attended.astype(jnp.float32), attend_readout, precision=lax.Precision.HIGHEST)
    score = score + jnp.dot(state_mixed.astype(jnp.float32), state_readout, precision=lax.Precision.HIGHEST)
    sums = jax.ops.segment_sum(score, segment_index, num_segments=SEGMENTS)
    counts = jax.ops.segment_sum(jnp.ones_like(score), segment_index, num_segments=SEGMENTS)
    return (attended, state_mixed, sums / counts)
```

```python
import functools
import math

import jax
import jax.numpy as jnp
from jax import lax
from jax.experimental import pallas as pl
from jax.experimental.pallas import tpu as pltpu
from jax.sharding import Mesh
from jax.sharding import PartitionSpec as P

HEADS = 64
KV_HEADS = 8
DIM = 128
BLOCK = 128
SEGMENTS = 32
COLUMNS = 8192
EPS = 1e-5

F32 = jnp.float32
BF16 = jnp.bfloat16
CTX = ("zl", "core")
HEAD = ("zh", "y", "x")
VMEM = pl.BlockSpec(memory_space=pltpu.VMEM)
SMEM = pl.BlockSpec(memory_space=pltpu.SMEM)
ANY = pl.BlockSpec(memory_space=pl.ANY)
NEG = -1e30
FADE = 2 * DIM
STATE_ROWS = FADE + 16


def call(kernel, outs, ins, scratch=(), flops=10**6, moved=10**6, mib=24):
    many = isinstance(outs, (tuple, list))
    return pl.pallas_call(
        kernel,
        out_shape=outs,
        in_specs=ins,
        out_specs=[VMEM] * len(outs) if many else VMEM,
        scratch_shapes=scratch,
        cost_estimate=pl.CostEstimate(flops=flops, bytes_accessed=moved, transcendentals=0),
        compiler_params=pltpu.CompilerParams(vmem_limit_bytes=mib * 2**20),
    )


def shape(dims, kind=F32):
    return jax.ShapeDtypeStruct(dims, kind)


def dot(a, b, ca=1, cb=0):
    return lax.dot_general(a, b, (((ca,), (cb,)), ((), ())), preferred_element_type=F32)


def split(v):
    high = v.astype(BF16)
    return high, (v - high.astype(F32)).astype(BF16)


def pack_kernel(k_ref, v_ref, o_ref, piece, sems):
    group = lax.axis_index("zh") * 4 + lax.axis_index("y")
    rows = pl.ds(pl.multiple_of(lax.axis_index("x") * 64, 64), 64)
    cols = pl.ds(pl.multiple_of(group * DIM, DIM), DIM)
    copies = [
        pltpu.make_async_copy(ref.at[rows, cols], piece.at[pl.ds(64 * n, 64)], sems.at[n])
        for n, ref in enumerate((k_ref, v_ref))
    ]
    for c in copies:
        c.start()
    for c in copies:
        c.wait()
    both = piece[...]
    for n in range(o_ref.shape[0]):
        o_ref[n] = both


def code_sums(codes_ref):
    rows = []
    for b in range(2):
        part = codes_ref[:, b * BLOCK : (b + 1) * BLOCK]
        rows += [part >> 6, part & 63]
    stacked = jnp.concatenate(rows, axis=0).astype(F32).astype(BF16)
    upto = lax.broadcasted_iota(jnp.int32, (BLOCK, BLOCK), 0) <= lax.broadcasted_iota(
        jnp.int32, (BLOCK, BLOCK), 1
    )
    total = dot(stacked, jnp.where(upto, 1.0, 0.0).astype(BF16))
    sums = {}
    for b in range(2):
        for h in range(2):
            sums[b, h] = 64.0 * total[4 * b + h : 4 * b + h + 1] + total[4 * b + 2 + h : 4 * b + 3 + h]
    return sums


def square(row):
    lanes = jnp.broadcast_to(row, (DIM, DIM))
    return lanes, jnp.transpose(lanes)


def states_kernel(x_ref, w_ref, codes_ref, rates_ref, own_ref, send_ref):
    sums = code_sums(codes_ref)
    row = lax.broadcasted_iota(jnp.int32, (8, DIM), 0)
    fades, marks = jnp.zeros((8, DIM), F32), jnp.zeros((8, DIM), F32)
    for h in range(2):
        cols = pl.ds(h * DIM, DIM)
        rate = rates_ref[h]
        state = None
        whole = None
        for b in range(2):
            rows = pl.ds(b * BLOCK, BLOCK)
            _, down = square(sums[b, h])
            last = down[BLOCK - 1 : BLOCK]
            tail = jnp.exp(rate * (down - last))
            written = (w_ref[rows, cols].astype(F32) * tail).astype(BF16)
            added = dot(written, x_ref[rows, cols], 0, 0)
            fade = jnp.exp(-rate * last)
            state = added if b == 0 else fade * state + added
            whole = last if b == 0 else whole + last
        own_ref[pl.ds(h * DIM, DIM)] = state
        send_ref[pl.ds(h * DIM, DIM)] = state.astype(BF16)
        fade = jnp.exp(-rate * whole)
        high = fade.astype(BF16).astype(F32)
        marks = jnp.where(row == h, fade, marks)
        fades = jnp.where(row == 2 * h, high, jnp.where(row == 2 * h + 1, fade - high, fades))
    own_ref[pl.ds(FADE, 8)] = marks
    send_ref[pl.ds(FADE, 16)] = jnp.concatenate([fades, jnp.zeros((8, DIM), F32)], axis=0).astype(BF16)


def first_kernel(got_ref, t_ref, t_out, x_out, send_ref):
    merge(got_ref, t_ref, None, t_out, x_out, send_ref)


def middle_kernel(got_ref, t_ref, x_ref, t_out, x_out, send_ref):
    merge(got_ref, t_ref, x_ref, t_out, x_out, send_ref)


def merge(got_ref, t_ref, x_ref, t_out, x_out, send_ref):
    got_fades = got_ref[pl.ds(FADE, 16)].astype(F32)
    row = lax.broadcasted_iota(jnp.int32, (8, DIM), 0)
    fades, marks_t, marks_x = (jnp.zeros((8, DIM), F32) for _ in range(3))
    for h in range(2):
        rows = pl.ds(h * DIM, DIM)
        got = got_ref[rows].astype(F32)
        got_fade = got_fades[2 * h : 2 * h + 1] + got_fades[2 * h + 1 : 2 * h + 2]
        mine = t_ref[pl.ds(FADE, 8)][h : h + 1]
        state = mine * got + t_ref[rows]
        t_out[rows] = state
        send_ref[rows] = state.astype(BF16)
        fade = mine * got_fade
        if x_ref is None:
            x_out[rows] = got
            x_fade = got_fade
        else:
            before = x_ref[pl.ds(FADE, 8)][h : h + 1]
            x_out[rows] = before * got + x_ref[rows]
            x_fade = before * got_fade
        high = fade.astype(BF16).astype(F32)
        marks_t = jnp.where(row == h, fade, marks_t)
        marks_x = jnp.where(row == h, x_fade, marks_x)
        fades = jnp.where(row == 2 * h, high, jnp.where(row == 2 * h + 1, fade - high, fades))
    t_out[pl.ds(FADE, 8)] = marks_t
    x_out[pl.ds(FADE, 8)] = marks_x
    send_ref[pl.ds(FADE, 16)] = jnp.concatenate([fades, jnp.zeros((8, DIM), F32)], axis=0).astype(BF16)


def local_kernel(x_ref, w_ref, r_ref, g_ref, codes_ref, rates_ref, skip_ref, base_ref, carry_ref):
    sums = code_sums(codes_ref)
    lower = lax.broadcasted_iota(jnp.int32, (BLOCK, BLOCK), 0) >= lax.broadcasted_iota(
        jnp.int32, (BLOCK, BLOCK), 1
    )
    for h in range(2):
        cols = pl.ds(h * DIM, DIM)
        rate, skip = rates_ref[h], skip_ref[h]
        state, before = None, None
        for b in range(2):
            rows = pl.ds(b * BLOCK, BLOCK)
            across, down = square(sums[b, h])
            x, w, r = x_ref[rows, cols], w_ref[rows, cols], r_ref[rows, cols]
            decay = jnp.exp(jnp.minimum(rate * (across - down), 0.0))
            scores = dot(r, w, 1, 1)
            mix = jnp.where(lower, scores * decay, 0.0).astype(BF16)
            y = dot(mix, x) + skip * x.astype(F32)
            if b == 0:
                last = down[BLOCK - 1 : BLOCK]
                tail = jnp.exp(rate * (down - last))
                state = dot((w.astype(F32) * tail).astype(BF16), x, 0, 0)
                before = last
                carry = jnp.exp(-rate * down)
            else:
                high, low = split(state)
                y = y + jnp.exp(-rate * down) * (dot(r, high) + dot(r, low))
                carry = jnp.exp(-rate * (down + before))
            gate = g_ref[rows, cols].astype(F32)
            silu = gate / (1.0 + jnp.exp(-gate))
            base_ref[rows, cols] = y * silu
            carry_ref[rows, cols] = carry * silu


def to_lanes(v):
    halves = v[:, :DIM] + v[:, DIM:]
    return [
        jnp.sum(jnp.transpose(halves[b * DIM : (b + 1) * DIM]), axis=0, keepdims=True)
        for b in range(2)
    ]


def carried_kernel(got_ref, x_ref, r_ref, base_ref, carry_ref, gain_ref, readout_ref, gated_ref, stat_ref):
    parts = []
    for h in range(2):
        rows, cols = pl.ds(h * DIM, DIM), pl.ds(h * DIM, DIM)
        before = x_ref[pl.ds(FADE, 8)][h : h + 1]
        entering = before * got_ref[rows].astype(F32) + x_ref[rows]
        high, low = split(entering)
        r = r_ref[:, cols]
        parts.append(base_ref[:, cols] + carry_ref[:, cols] * (dot(r, high) + dot(r, low)))
    gated = jnp.concatenate(parts, axis=1)
    gated_ref[...] = gated
    weight = gain_ref[...] * readout_ref[...]
    stat_ref[...] = jnp.concatenate(to_lanes(gated * gated) + to_lanes(gated * weight), axis=0)


def attend_kernel(q_ref, *refs):
    own, other = refs[0:4], refs[4:8]
    readout_ref, stat_ref, o_ref, send_ref, m_ref, l_ref, acc_ref = refs[8:]
    zl, core, x = (lax.axis_index(a) for a in ("zl", "core", "x"))
    m_ref[...] = jnp.full(m_ref.shape, NEG, F32)
    l_ref[...] = jnp.zeros(l_ref.shape, F32)
    acc_ref[...] = jnp.zeros(acc_ref.shape, F32)
    c = math.log2(math.e) / math.sqrt(DIM)

    def tile(k, masked):
        keys = jnp.concatenate([ref[k, 0:64] for ref in own + other], axis=0)
        values = jnp.concatenate([ref[k, 64:128] for ref in own + other], axis=0)
        width = keys.shape[0]
        if masked:
            lane = lax.broadcasted_iota(jnp.int32, (128, 128), 1)
            place = []
            for n in range(2):
                first = jnp.bitwise_xor(x, 2 * n) * 64
                second = jnp.bitwise_xor(x, 2 * n + 1) * 64 - 64
                place.append(lane + jnp.where(lane < 64, first, second))
            far = jnp.full((128, 128), jnp.where(core == 1, 0, 1 << 20), jnp.int32)
            place = jnp.concatenate(place + [far, far], axis=1)
        for h in range(2):
            for n in range(2):
                rows = pl.ds(n * 128, 128)
                at = pl.ds(h * 256 + n * 128, 128)
                s = dot(q_ref[rows, pl.ds(h * DIM, DIM)], keys, 1, 1)
                if masked:
                    spot = lax.broadcasted_iota(jnp.int32, (128, width), 0) + n * 128
                    s = jnp.where(place <= spot, s, NEG)
                old = m_ref[at]
                peak = jnp.max(s, axis=1, keepdims=True)
                new = jnp.maximum(old, peak)
                fade = jnp.exp2((old - new) * c)
                m_ref[at] = new
                p = jnp.concatenate(
                    [jnp.exp2((s[:, i : i + 128] - new) * c) for i in range(0, width, 128)], axis=1
                )
                part = p[:, 0:128]
                for i in range(128, width, 128):
                    part = part + p[:, i : i + 128]
                l_ref[at] = l_ref[at] * fade + part
                acc_ref[at] = acc_ref[at] * fade + dot(p.astype(BF16), values)

    def full(k, _):
        tile(k, False)
        return 0

    lax.fori_loop(0, zl, full, 0)
    tile(zl, True)
    parts = []
    for h in range(2):
        at = pl.ds(h * 256, 256)
        parts.append(acc_ref[at] / jnp.sum(l_ref[at], axis=1, keepdims=True))
    attended = jnp.concatenate(parts, axis=1).astype(BF16)
    o_ref[...] = attended
    a = to_lanes(attended.astype(F32) * readout_ref[...])
    stats = jnp.concatenate([stat_ref[...]] + a + [jnp.zeros((2, DIM), F32)], axis=0)
    for n in range(send_ref.shape[0]):
        send_ref[n] = stats


def segment_row(values):
    full = jnp.concatenate([values, jnp.zeros((DIM - SEGMENTS, DIM), F32)], axis=0)
    return jnp.sum(jnp.transpose(full), axis=0, keepdims=True)


def middle_sums_kernel(got_ref, seg_ref, send_ref):
    total = got_ref[0]
    for n in range(1, got_ref.shape[0]):
        total = total + got_ref[n]
    segment = lax.broadcasted_iota(jnp.int32, (SEGMENTS, DIM), 0)
    seg = seg_ref[...]
    part = jnp.zeros((SEGMENTS, DIM), F32)
    for j in range(2):
        part = part + jnp.where(seg[j : j + 1] == segment, total[4 + j : 5 + j], 0.0)
    part = segment_row(part)
    high = part.astype(BF16).astype(F32)
    out = jnp.concatenate([total[0:4], high, part - high, seg.astype(F32)], axis=0).astype(BF16)
    for n in range(send_ref.shape[0]):
        send_ref[n] = out


def final_kernel(got_ref, gated_ref, gain_ref, o_ref, values_ref):
    index = lax.axis_index("zl") * 2 + lax.axis_index("core")
    mine = got_ref[2 * index].astype(F32) + got_ref[2 * index + 1].astype(F32)
    gain = gain_ref[...]
    for b in range(2):
        rows = pl.ds(b * DIM, DIM)
        scale = lax.rsqrt(mine[b : b + 1] * (1.0 / COLUMNS) + EPS)
        _, down = square(scale)
        for h in range(2):
            cols = slice(h * DIM, (h + 1) * DIM)
            o_ref[rows, cols] = (gated_ref[rows, cols] * down * gain[:, cols]).astype(BF16)
    segment = lax.broadcasted_iota(jnp.int32, (SEGMENTS, DIM), 0)
    part = jnp.zeros((SEGMENTS, DIM), F32)
    count = jnp.zeros((SEGMENTS, DIM), F32)
    extra = jnp.zeros((8, DIM), F32)
    for s in range(got_ref.shape[0] // 2):
        low = got_ref[2 * s].astype(F32)
        both = low + got_ref[2 * s + 1].astype(F32)
        extra = extra + both
        scale = lax.rsqrt(both[0:2] * (1.0 / COLUMNS) + EPS)
        score = scale * both[2:4]
        seg = low[6:8].astype(jnp.int32)
        for j in range(2):
            member = seg[j : j + 1] == segment
            part = part + jnp.where(member, score[j : j + 1], 0.0)
            count = count + jnp.where(member, 1.0, 0.0)
    total = segment_row(part) + extra[4:5] + extra[5:6]
    held = segment_row(count)
    values_ref[...] = (total / jnp.maximum(held, 1.0))[:, :SEGMENTS]


def per_device(
    queries,
    key_rows,
    value_rows,
    state_input,
    state_write,
    state_read,
    gate_input,
    decay_codes,
    decay_rates,
    skip_gain,
    norm_gain,
    attend_readout,
    state_readout,
    segment_index,
):
    tokens = queries.shape[0]
    codes = decay_codes.T
    seg = segment_index.reshape(2, DIM)
    gain = norm_gain.reshape(1, 256)
    state_out = state_readout.reshape(1, 256)
    attend_out = attend_readout.reshape(1, 256)
    chips, wide = lax.axis_size("zl"), lax.axis_size("x")
    ctx = chips * lax.axis_size("core")

    packed = call(
        pack_kernel,
        shape((chips, DIM, DIM), BF16),
        [ANY, ANY],
        [pltpu.VMEM((DIM, DIM), BF16), pltpu.SemaphoreType.DMA((2,))],
    )(key_rows, value_rows)
    quarter = lax.all_to_all(packed, "zl", 0, 0)

    state_shapes = (shape((FADE + 8, DIM)), shape((STATE_ROWS, DIM), BF16))
    own, send = call(states_kernel, state_shapes, [VMEM, VMEM, VMEM, SMEM])(
        state_input, state_write, codes, decay_rates
    )

    def shifted(v, by):
        return lax.ppermute(v, CTX, [(i, i + by) for i in range(ctx - by)])

    merged = (shape((FADE + 8, DIM)), shape((FADE + 8, DIM)), shape((STATE_ROWS, DIM), BF16))
    got = shifted(send, 1)
    t, before, send = call(first_kernel, merged, [VMEM] * 2)(got, own)
    got = shifted(send, 2)
    base, carry = call(
        local_kernel, (shape((tokens, 256)), shape((tokens, 256))), [VMEM] * 5 + [SMEM] * 2
    )(state_input, state_write, state_read, gate_input, codes, decay_rates, skip_gain)
    t, before, send = call(middle_kernel, merged, [VMEM] * 3)(got, t, before)
    got = shifted(send, 4)
    t, before, send = call(middle_kernel, merged, [VMEM] * 3)(got, t, before)
    got = shifted(send, 8)

    pieces = [quarter] + [
        lax.ppermute(quarter, "x", [(i, i ^ k) for i in range(wide)]) for k in range(1, wide)
    ]
    others = [lax.ppermute(p, "core", [(0, 1), (1, 0)]) for p in pieces]

    gated, stats = call(
        carried_kernel, (shape((tokens, 256)), shape((4, DIM))), [VMEM] * 7
    )(got, before, state_read, base, carry, gain, state_out)

    head_plane = lax.axis_size("y") * wide
    attended, send = call(
        attend_kernel,
        (shape((tokens, 256), BF16), shape((head_plane, 8, DIM))),
        [VMEM] * 11,
        [pltpu.VMEM((512, DIM), F32) for _ in range(3)],
    )(queries, *pieces, *others, attend_out, stats)
    summed = lax.all_to_all(send, ("y", "x"), 0, 0)
    line = ctx * lax.axis_size("zh")
    send = call(middle_sums_kernel, shape((line, 8, DIM), BF16), [VMEM] * 2)(summed, seg)
    summed = lax.all_to_all(send, ("zl", "core", "zh"), 0, 0)
    state_mixed, values = call(
        final_kernel, (shape((tokens, 256), BF16), shape((1, SEGMENTS))), [VMEM] * 3
    )(summed, gated, gain)
    return attended, state_mixed, values.reshape(SEGMENTS)


def solution(mesh):
    grid = mesh.devices.shape
    inner = Mesh(mesh.devices.reshape(grid[0] // 2, 2, 2, 4, grid[1] // 8), CTX + HEAD)
    both = P(CTX, HEAD)
    rows, heads = P(CTX), P(HEAD)
    in_specs = (both, P(CTX, None), P(CTX, None)) + (both,) * 5 + (heads,) * 5 + (rows,)
    return jax.shard_map(
        per_device, mesh=inner, in_specs=in_specs, out_specs=(both, both, P()), check_vma=False
    )
```

```python
import functools
import math

import jax
import jax.numpy as jnp
from jax import lax
from jax.experimental import pallas as pl
from jax.experimental.pallas import tpu as pltpu
from jax.sharding import Mesh
from jax.sharding import PartitionSpec as P

HEADS = 64
KV_HEADS = 8
DIM = 128
BLOCK = 128
SEGMENTS = 32
COLUMNS = 8192
EPS = 1e-5

F32 = jnp.float32
BF16 = jnp.bfloat16
CTX = ("zl", "core")
HEAD = ("zh", "y", "x")
VMEM = pl.BlockSpec(memory_space=pltpu.VMEM)
SMEM = pl.BlockSpec(memory_space=pltpu.SMEM)
HBM = pl.BlockSpec(memory_space=pltpu.HBM)
NEG = -1e30
FADE = 2 * DIM
STATE_ROWS = FADE + 16


def call(kernel, outs, ins, scratch=(), flops=10**6, moved=10**6, mib=24):
    many = isinstance(outs, (tuple, list))
    return pl.pallas_call(
        kernel,
        out_shape=outs,
        in_specs=ins,
        out_specs=[VMEM] * len(outs) if many else VMEM,
        scratch_shapes=scratch,
        cost_estimate=pl.CostEstimate(flops=flops, bytes_accessed=moved, transcendentals=0),
        compiler_params=pltpu.CompilerParams(vmem_limit_bytes=mib * 2**20),
    )


def shape(dims, kind=F32):
    return jax.ShapeDtypeStruct(dims, kind)


def dot(a, b, ca=1, cb=0):
    return lax.dot_general(a, b, (((ca,), (cb,)), ((), ())), preferred_element_type=F32)


def split(v):
    high = v.astype(BF16)
    return high, (v - high.astype(F32)).astype(BF16)


def pack_kernel(k_ref, v_ref, o_ref, piece, sems):
    group = lax.axis_index("zh") * 4 + lax.axis_index("y")
    rows = pl.ds(pl.multiple_of(lax.axis_index("x") * 64, 64), 64)
    cols = pl.ds(pl.multiple_of(group * DIM, DIM), DIM)
    copies = [
        pltpu.make_async_copy(ref.at[rows, cols], piece.at[pl.ds(64 * n, 64)], sems.at[n])
        for n, ref in enumerate((k_ref, v_ref))
    ]
    for c in copies:
        c.start()
    for c in copies:
        c.wait()
    both = piece[...]
    for n in range(o_ref.shape[0]):
        o_ref[n] = both


def code_sums(codes_ref):
    rows = []
    for b in range(2):
        part = codes_ref[:, b * BLOCK : (b + 1) * BLOCK]
        rows += [part >> 6, part & 63]
    stacked = jnp.concatenate(rows, axis=0).astype(F32).astype(BF16)
    upto = lax.broadcasted_iota(jnp.int32, (BLOCK, BLOCK), 0) <= lax.broadcasted_iota(
        jnp.int32, (BLOCK, BLOCK), 1
    )
    total = dot(stacked, jnp.where(upto, 1.0, 0.0).astype(BF16))
    sums = {}
    for b in range(2):
        for h in range(2):
            sums[b, h] = 64.0 * total[4 * b + h : 4 * b + h + 1] + total[4 * b + 2 + h : 4 * b + 3 + h]
    return sums


def square(row):
    lanes = jnp.broadcast_to(row, (DIM, DIM))
    return lanes, jnp.transpose(lanes)


def states_kernel(x_ref, w_ref, codes_ref, rates_ref, own_ref, send_ref):
    sums = code_sums(codes_ref)
    row = lax.broadcasted_iota(jnp.int32, (8, DIM), 0)
    fades, marks = jnp.zeros((8, DIM), F32), jnp.zeros((8, DIM), F32)
    for h in range(2):
        cols = pl.ds(h * DIM, DIM)
        rate = rates_ref[h]
        state = None
        whole = None
        for b in range(2):
            rows = pl.ds(b * BLOCK, BLOCK)
            _, down = square(sums[b, h])
            last = down[BLOCK - 1 : BLOCK]
            tail = jnp.exp(rate * (down - last))
            written = (w_ref[rows, cols].astype(F32) * tail).astype(BF16)
            added = dot(written, x_ref[rows, cols], 0, 0)
            fade = jnp.exp(-rate * last)
            state = added if b == 0 else fade * state + added
            whole = last if b == 0 else whole + last
        own_ref[pl.ds(h * DIM, DIM)] = state
        send_ref[pl.ds(h * DIM, DIM)] = state.astype(BF16)
        fade = jnp.exp(-rate * whole)
        high = fade.astype(BF16).astype(F32)
        marks = jnp.where(row == h, fade, marks)
        fades = jnp.where(row == 2 * h, high, jnp.where(row == 2 * h + 1, fade - high, fades))
    own_ref[pl.ds(FADE, 8)] = marks
    send_ref[pl.ds(FADE, 16)] = jnp.concatenate([fades, jnp.zeros((8, DIM), F32)], axis=0).astype(BF16)


def first_kernel(got_ref, t_ref, quarter_ref, t_out, x_out, send_ref, fan_ref):
    for n in range(fan_ref.shape[0]):
        fan_ref[n] = quarter_ref[...]
    merge(got_ref, t_ref, None, t_out, x_out, send_ref)


def middle_kernel(got_ref, t_ref, x_ref, t_out, x_out, send_ref):
    merge(got_ref, t_ref, x_ref, t_out, x_out, send_ref)


def merge(got_ref, t_ref, x_ref, t_out, x_out, send_ref):
    got_fades = got_ref[pl.ds(FADE, 16)].astype(F32)
    row = lax.broadcasted_iota(jnp.int32, (8, DIM), 0)
    fades, marks_t, marks_x = (jnp.zeros((8, DIM), F32) for _ in range(3))
    for h in range(2):
        rows = pl.ds(h * DIM, DIM)
        got = got_ref[rows].astype(F32)
        got_fade = got_fades[2 * h : 2 * h + 1] + got_fades[2 * h + 1 : 2 * h + 2]
        mine = t_ref[pl.ds(FADE, 8)][h : h + 1]
        state = mine * got + t_ref[rows]
        t_out[rows] = state
        send_ref[rows] = state.astype(BF16)
        fade = mine * got_fade
        if x_ref is None:
            x_out[rows] = got
            x_fade = got_fade
        else:
            before = x_ref[pl.ds(FADE, 8)][h : h + 1]
            x_out[rows] = before * got + x_ref[rows]
            x_fade = before * got_fade
        high = fade.astype(BF16).astype(F32)
        marks_t = jnp.where(row == h, fade, marks_t)
        marks_x = jnp.where(row == h, x_fade, marks_x)
        fades = jnp.where(row == 2 * h, high, jnp.where(row == 2 * h + 1, fade - high, fades))
    t_out[pl.ds(FADE, 8)] = marks_t
    x_out[pl.ds(FADE, 8)] = marks_x
    send_ref[pl.ds(FADE, 16)] = jnp.concatenate([fades, jnp.zeros((8, DIM), F32)], axis=0).astype(BF16)


def local_kernel(x_ref, w_ref, r_ref, g_ref, codes_ref, rates_ref, skip_ref, base_ref, carry_ref):
    sums = code_sums(codes_ref)
    lower = lax.broadcasted_iota(jnp.int32, (BLOCK, BLOCK), 0) >= lax.broadcasted_iota(
        jnp.int32, (BLOCK, BLOCK), 1
    )
    for h in range(2):
        cols = pl.ds(h * DIM, DIM)
        rate, skip = rates_ref[h], skip_ref[h]
        state, before = None, None
        for b in range(2):
            rows = pl.ds(b * BLOCK, BLOCK)
            across, down = square(sums[b, h])
            x, w, r = x_ref[rows, cols], w_ref[rows, cols], r_ref[rows, cols]
            decay = jnp.exp(jnp.minimum(rate * (across - down), 0.0))
            scores = dot(r, w, 1, 1)
            mix = jnp.where(lower, scores * decay, 0.0).astype(BF16)
            y = dot(mix, x) + skip * x.astype(F32)
            if b == 0:
                last = down[BLOCK - 1 : BLOCK]
                tail = jnp.exp(rate * (down - last))
                state = dot((w.astype(F32) * tail).astype(BF16), x, 0, 0)
                before = last
                carry = jnp.exp(-rate * down)
            else:
                high, low = split(state)
                y = y + jnp.exp(-rate * down) * (dot(r, high) + dot(r, low))
                carry = jnp.exp(-rate * (down + before))
            gate = g_ref[rows, cols].astype(F32)
            silu = gate / (1.0 + jnp.exp(-gate))
            base_ref[rows, cols] = y * silu
            carry_ref[rows, cols] = carry * silu


def to_lanes(v):
    halves = v[:, :DIM] + v[:, DIM:]
    return [
        jnp.sum(jnp.transpose(halves[b * DIM : (b + 1) * DIM]), axis=0, keepdims=True)
        for b in range(2)
    ]


def carried_kernel(
    got_ref, x_ref, r_ref, base_ref, carry_ref, gain_ref, readout_ref, a_ref, gated_ref, send_ref
):
    parts = []
    for h in range(2):
        rows, cols = pl.ds(h * DIM, DIM), pl.ds(h * DIM, DIM)
        before = x_ref[pl.ds(FADE, 8)][h : h + 1]
        entering = before * got_ref[rows].astype(F32) + x_ref[rows]
        high, low = split(entering)
        r = r_ref[:, cols]
        parts.append(base_ref[:, cols] + carry_ref[:, cols] * (dot(r, high) + dot(r, low)))
    gated = jnp.concatenate(parts, axis=1)
    gated_ref[...] = gated
    weight = gain_ref[...] * readout_ref[...]
    stats = to_lanes(gated * gated) + to_lanes(gated * weight)
    stats = jnp.concatenate(stats + [a_ref[...], jnp.zeros((2, DIM), F32)], axis=0)
    for n in range(send_ref.shape[0]):
        send_ref[n] = stats


def keys_of(ref, k):
    return jnp.concatenate([ref[n, k + i, 0:64] for i in range(2) for n in range(4)], axis=0)


def values_of(ref, k):
    return jnp.concatenate([ref[n, k + i, 64:128] for i in range(2) for n in range(4)], axis=0)


def spread(q_ref, scaled_ref):
    c = math.log2(math.e) / math.sqrt(DIM)
    for h in range(2):
        high, low = split(q_ref[:, h * DIM : (h + 1) * DIM].astype(F32) * c)
        scaled_ref[pl.ds(h * 256, 256)] = jnp.concatenate([high, low], axis=1)


def scan_keys(kv_ref, core, scaled_ref, scores_ref, m_ref, l_ref, acc_ref, fresh):
    zl, here = lax.axis_index("zl"), lax.axis_index("core")
    tiles = zl + 1 if fresh else zl + here
    pairs = zl // 2 if fresh else tiles // 2
    rows = scaled_ref.shape[0]

    def lanes_max(s):
        return jnp.maximum(
            jnp.maximum(s[:, 0:128], s[:, 128:256]), jnp.maximum(s[:, 256:384], s[:, 384:512])
        )

    def scores(i):
        keys = keys_of(kv_ref, 2 * i)
        return dot(scaled_ref[...], jnp.concatenate([keys, keys], axis=1), 1, 1)

    def first(i, _):
        s = scores(i)
        scores_ref[i] = s
        m_ref[...] = jnp.maximum(m_ref[...], lanes_max(s))
        return 0

    def tail(i):
        key = lax.broadcasted_iota(jnp.int32, (rows, 512), 1)
        key = (i * 2) * 512 + core * 256 + jnp.where(key < 256, key, key + 256)
        spot = lax.broadcasted_iota(jnp.int32, (rows, 512), 0)
        spot = zl * 512 + here * 256 + jnp.where(spot < 256, spot, spot - 256)
        s = jnp.where(key <= spot, scores(i), NEG)
        scores_ref[i] = s
        m_ref[...] = jnp.maximum(m_ref[...], lanes_max(s))

    old = m_ref[...]
    lax.fori_loop(0, pairs, first, 0)
    ragged = 2 * pairs < tiles

    @pl.when(ragged)
    def _():
        tail(pairs)

    top = jnp.broadcast_to(jnp.max(m_ref[...], axis=1, keepdims=True), m_ref.shape)
    if fresh:
        l_ref[...] = jnp.zeros(l_ref.shape, F32)
        acc_ref[...] = jnp.zeros(acc_ref.shape, F32)
    else:
        fade = jnp.exp2(old - top)
        l_ref[...] = l_ref[...] * fade
        acc_ref[...] = acc_ref[...] * fade
    m_ref[...] = top

    def second(i, _):
        top = m_ref[...]
        p = [jnp.exp2(scores_ref[i, :, n : n + 128] - top) for n in range(0, 512, 128)]
        l_ref[...] += (p[0] + p[1]) + (p[2] + p[3])
        weights = jnp.concatenate([v.astype(BF16) for v in p], axis=1)
        acc_ref[...] += dot(weights, values_of(kv_ref, 2 * i))
        return 0

    lax.fori_loop(0, pairs + ragged.astype(jnp.int32), second, 0)


def attend_own_kernel(q_ref, kv_ref, scaled_ref, m_ref, l_ref, acc_ref, scores_ref):
    spread(q_ref, scaled_ref)
    m_ref[...] = jnp.full(m_ref.shape, NEG, F32)
    scan_keys(kv_ref, lax.axis_index("core"), scaled_ref, scores_ref, m_ref, l_ref, acc_ref, True)


def attend_other_kernel(
    scaled_ref, kv_ref, m_in, l_in, acc_in, readout_ref, o_ref, a_ref, m_ref, l_ref, acc_ref, scores_ref
):
    m_ref[...] = m_in[...]
    l_ref[...] = l_in[...]
    acc_ref[...] = acc_in[...]
    other = 1 - lax.axis_index("core")
    scan_keys(kv_ref, other, scaled_ref, scores_ref, m_ref, l_ref, acc_ref, False)
    parts = []
    for h in range(2):
        at = pl.ds(h * 256, 256)
        parts.append(acc_ref[at] / jnp.sum(l_ref[at], axis=1, keepdims=True))
    attended = jnp.concatenate(parts, axis=1).astype(BF16)
    o_ref[...] = attended
    a_ref[...] = jnp.concatenate(to_lanes(attended.astype(F32) * readout_ref[...]), axis=0)


def segment_row(values):
    full = jnp.concatenate([values, jnp.zeros((DIM - SEGMENTS, DIM), F32)], axis=0)
    return jnp.sum(jnp.transpose(full), axis=0, keepdims=True)


def middle_sums_kernel(got_ref, seg_ref, send_ref):
    total = got_ref[0]
    for n in range(1, got_ref.shape[0]):
        total = total + got_ref[n]
    segment = lax.broadcasted_iota(jnp.int32, (SEGMENTS, DIM), 0)
    seg = seg_ref[...]
    part = jnp.zeros((SEGMENTS, DIM), F32)
    for j in range(2):
        part = part + jnp.where(seg[j : j + 1] == segment, total[4 + j : 5 + j], 0.0)
    part = segment_row(part)
    high = part.astype(BF16).astype(F32)
    out = jnp.concatenate([total[0:4], high, part - high, seg.astype(F32)], axis=0).astype(BF16)
    for n in range(send_ref.shape[0]):
        send_ref[n] = out


def final_kernel(got_ref, gated_ref, gain_ref, o_ref, values_ref):
    index = lax.axis_index("zl") * 2 + lax.axis_index("core")
    mine = got_ref[2 * index].astype(F32) + got_ref[2 * index + 1].astype(F32)
    gain = gain_ref[...]
    for b in range(2):
        rows = pl.ds(b * DIM, DIM)
        scale = lax.rsqrt(mine[b : b + 1] * (1.0 / COLUMNS) + EPS)
        _, down = square(scale)
        for h in range(2):
            cols = slice(h * DIM, (h + 1) * DIM)
            o_ref[rows, cols] = (gated_ref[rows, cols] * down * gain[:, cols]).astype(BF16)
    segment = lax.broadcasted_iota(jnp.int32, (SEGMENTS, DIM), 0)
    part = jnp.zeros((SEGMENTS, DIM), F32)
    count = jnp.zeros((SEGMENTS, DIM), F32)
    extra = jnp.zeros((8, DIM), F32)
    for s in range(got_ref.shape[0] // 2):
        low = got_ref[2 * s].astype(F32)
        both = low + got_ref[2 * s + 1].astype(F32)
        extra = extra + both
        scale = lax.rsqrt(both[0:2] * (1.0 / COLUMNS) + EPS)
        score = scale * both[2:4]
        seg = low[6:8].astype(jnp.int32)
        for j in range(2):
            member = seg[j : j + 1] == segment
            part = part + jnp.where(member, score[j : j + 1], 0.0)
            count = count + jnp.where(member, 1.0, 0.0)
    total = segment_row(part) + extra[4:5] + extra[5:6]
    held = segment_row(count)
    values_ref[...] = (total / jnp.maximum(held, 1.0))[:, :SEGMENTS]


def per_device(
    queries,
    key_rows,
    value_rows,
    state_input,
    state_write,
    state_read,
    gate_input,
    decay_codes,
    decay_rates,
    skip_gain,
    norm_gain,
    attend_readout,
    state_readout,
    segment_index,
):
    tokens = queries.shape[0]
    codes = decay_codes.T
    seg = segment_index.reshape(2, DIM)
    gain = norm_gain.reshape(1, 256)
    state_out = state_readout.reshape(1, 256)
    attend_out = attend_readout.reshape(1, 256)
    chips, wide = lax.axis_size("zl"), lax.axis_size("x")
    ctx = chips * lax.axis_size("core")

    together = lax.optimization_barrier
    state_shapes = (shape((FADE + 8, DIM)), shape((STATE_ROWS, DIM), BF16))
    own, send = call(states_kernel, state_shapes, [VMEM, VMEM, VMEM, SMEM])(
        state_input, state_write, codes, decay_rates
    )
    packed = call(
        pack_kernel,
        shape((chips, DIM, DIM), BF16),
        [HBM, HBM],
        [pltpu.VMEM((DIM, DIM), BF16), pltpu.SemaphoreType.DMA((2,))],
        mib=60,
    )(key_rows, value_rows)
    send, packed = together((send, packed))

    def shifted(v, by):
        return lax.ppermute(v, CTX, [(i, i + by) for i in range(ctx - by)])

    got = shifted(send, 1)
    quarter = lax.all_to_all(packed, "zl", 0, 0)
    got, quarter = together((got, quarter))
    merged = (shape((FADE + 8, DIM)), shape((FADE + 8, DIM)), shape((STATE_ROWS, DIM), BF16))
    fan_shape = shape((wide, chips, DIM, DIM), BF16)
    t, before, send, fan = call(first_kernel, merged + (fan_shape,), [VMEM] * 3)(got, own, quarter)

    got = shifted(send, 2)
    mine = lax.all_to_all(fan, "x", 0, 0)
    got, mine = together((got, mine))
    t, before, send = call(middle_kernel, merged, [VMEM] * 3)(got, t, before)
    send, mine = together((send, mine))

    got = shifted(send, 4)
    theirs = lax.ppermute(mine, "core", [(0, 1), (1, 0)])
    running = (shape((512, 256), BF16),) + (shape((512, DIM)),) * 3
    scores = pltpu.VMEM((chips // 2, 512, 512), F32)
    attention = call(attend_own_kernel, running, [VMEM] * 2, [scores], flops=10**9)(queries, mine)
    got, attention = together((got, attention))
    t, before, send = call(middle_kernel, merged, [VMEM] * 3)(got, t, before)
    send, theirs, attention, codes = together((send, theirs, attention, codes))

    got = shifted(send, 8)
    attended, a = call(
        attend_other_kernel,
        (shape((tokens, 256), BF16), shape((2, DIM))),
        [VMEM] * 6,
        [pltpu.VMEM((512, DIM), F32) for _ in range(3)] + [scores],
        flops=10**9,
    )(attention[0], theirs, *attention[1:], attend_out)
    base, carry = call(
        local_kernel, (shape((tokens, 256)), shape((tokens, 256))), [VMEM] * 5 + [SMEM] * 2
    )(state_input, state_write, state_read, gate_input, codes, decay_rates, skip_gain)
    got, a, base = together((got, a, base))
    head_plane = lax.axis_size("y") * wide
    gated, send = call(
        carried_kernel, (shape((tokens, 256)), shape((head_plane, 8, DIM))), [VMEM] * 8
    )(got, before, state_read, base, carry, gain, state_out, a)
    summed = lax.all_to_all(send, ("y", "x"), 0, 0)
    line = ctx * lax.axis_size("zh")
    send = call(middle_sums_kernel, shape((line, 8, DIM), BF16), [VMEM] * 2)(summed, seg)
    summed = lax.all_to_all(send, ("zl", "core", "zh"), 0, 0)
    state_mixed, values = call(
        final_kernel, (shape((tokens, 256), BF16), shape((1, SEGMENTS))), [VMEM] * 3
    )(summed, gated, gain)
    return attended, state_mixed, values.reshape(SEGMENTS)


def solution(mesh):
    grid = mesh.devices.shape
    inner = Mesh(mesh.devices.reshape(grid[0] // 2, 2, 2, 4, grid[1] // 8), CTX + HEAD)
    both = P(CTX, HEAD)
    rows, heads = P(CTX), P(HEAD)
    in_specs = (both, P(CTX, None), P(CTX, None)) + (both,) * 5 + (heads,) * 5 + (rows,)
    return jax.shard_map(
        per_device, mesh=inner, in_specs=in_specs, out_specs=(both, both, P()), check_vma=False
    )
```

```python
import functools
import math

import jax
import jax.numpy as jnp
from jax import lax
from jax.experimental import pallas as pl
from jax.experimental.pallas import tpu as pltpu
from jax.sharding import Mesh
from jax.sharding import PartitionSpec as P

HEADS = 64
KV_HEADS = 8
DIM = 128
BLOCK = 128
SEGMENTS = 32
COLUMNS = 8192
EPS = 1e-5

F32 = jnp.float32
BF16 = jnp.bfloat16
CTX = ("zl", "core")
HEAD = ("zh", "y", "x")
VMEM = pl.BlockSpec(memory_space=pltpu.VMEM)
SMEM = pl.BlockSpec(memory_space=pltpu.SMEM)
HBM = pl.BlockSpec(memory_space=pltpu.HBM)
NEG = -1e30
FADE = 2 * DIM
STATE_ROWS = FADE + 16


def call(kernel, outs, ins, scratch=(), flops=10**6, moved=10**6, mib=24):
    many = isinstance(outs, (tuple, list))
    return pl.pallas_call(
        kernel,
        out_shape=outs,
        in_specs=ins,
        out_specs=[VMEM] * len(outs) if many else VMEM,
        scratch_shapes=scratch,
        cost_estimate=pl.CostEstimate(flops=flops, bytes_accessed=moved, transcendentals=0),
        compiler_params=pltpu.CompilerParams(vmem_limit_bytes=int(mib * 2**20)),
    )


def shape(dims, kind=F32):
    return jax.ShapeDtypeStruct(dims, kind)


def dot(a, b, ca=1, cb=0):
    return lax.dot_general(a, b, (((ca,), (cb,)), ((), ())), preferred_element_type=F32)


def split(v):
    high = v.astype(BF16)
    return high, (v - high.astype(F32)).astype(BF16)


def code_sums(codes_ref):
    rows = []
    for b in range(2):
        part = codes_ref[:, b * BLOCK : (b + 1) * BLOCK]
        rows += [part >> 6, part & 63]
    stacked = jnp.concatenate(rows, axis=0).astype(F32).astype(BF16)
    upto = lax.broadcasted_iota(jnp.int32, (BLOCK, BLOCK), 0) <= lax.broadcasted_iota(
        jnp.int32, (BLOCK, BLOCK), 1
    )
    total = dot(stacked, jnp.where(upto, 1.0, 0.0).astype(BF16))
    sums = {}
    for b in range(2):
        for h in range(2):
            sums[b, h] = 64.0 * total[4 * b + h : 4 * b + h + 1] + total[4 * b + 2 + h : 4 * b + 3 + h]
    return sums


def square(row):
    lanes = jnp.broadcast_to(row, (DIM, DIM))
    return lanes, jnp.transpose(lanes)


def entry_kernel(
    x_ref, w_ref, codes_ref, rates_ref, k_ref, v_ref, gain_ref, state_out_ref, attend_out_ref, seg_ref,
    own_ref, send_ref, packed_ref, rows_ref, seg_out, piece, sems,
):
    group = lax.axis_index("zh") * 4 + lax.axis_index("y")
    quarter = pl.ds(pl.multiple_of(lax.axis_index("x") * 64, 64), 64)
    columns = pl.ds(pl.multiple_of(group * DIM, DIM), DIM)
    copies = [
        pltpu.make_async_copy(ref.at[quarter, columns], piece.at[pl.ds(64 * n, 64)], sems.at[n])
        for n, ref in enumerate((k_ref, v_ref))
    ]
    for c in copies:
        c.start()
    gain = gain_ref[...]
    rows_ref[...] = jnp.concatenate(
        [gain, gain * state_out_ref[...], attend_out_ref[...], jnp.zeros((5, 256), F32)], axis=0
    )
    seg_out[...] = seg_ref[...]
    sums = code_sums(codes_ref)
    row = lax.broadcasted_iota(jnp.int32, (8, DIM), 0)
    fades, marks = jnp.zeros((8, DIM), F32), jnp.zeros((8, DIM), F32)
    for h in range(2):
        cols = pl.ds(h * DIM, DIM)
        rate = rates_ref[h]
        state = None
        whole = None
        for b in range(2):
            rows = pl.ds(b * BLOCK, BLOCK)
            _, down = square(sums[b, h])
            last = down[BLOCK - 1 : BLOCK]
            tail = jnp.exp(rate * (down - last))
            written = (w_ref[rows, cols].astype(F32) * tail).astype(BF16)
            added = dot(written, x_ref[rows, cols], 0, 0)
            fade = jnp.exp(-rate * last)
            state = added if b == 0 else fade * state + added
            whole = last if b == 0 else whole + last
        own_ref[pl.ds(h * DIM, DIM)] = state
        send_ref[pl.ds(h * DIM, DIM)] = state.astype(BF16)
        fade = jnp.exp(-rate * whole)
        high = fade.astype(BF16).astype(F32)
        marks = jnp.where(row == h, fade, marks)
        fades = jnp.where(row == 2 * h, high, jnp.where(row == 2 * h + 1, fade - high, fades))
    own_ref[pl.ds(FADE, 8)] = marks
    send_ref[pl.ds(FADE, 16)] = jnp.concatenate([fades, jnp.zeros((8, DIM), F32)], axis=0).astype(BF16)
    for c in copies:
        c.wait()
    both = piece[...]
    for n in range(packed_ref.shape[0]):
        packed_ref[n] = both


def first_kernel(got_ref, t_ref, t_out, x_out, send_ref):
    merge(got_ref, t_ref, None, t_out, x_out, send_ref)


def fan_kernel(got_ref, t_ref, x_ref, quarter_ref, t_out, x_out, send_ref, fan_ref):
    for n in range(fan_ref.shape[0]):
        fan_ref[n] = quarter_ref[...]
    merge(got_ref, t_ref, x_ref, t_out, x_out, send_ref)


def middle_kernel(got_ref, t_ref, x_ref, t_out, x_out, send_ref):
    merge(got_ref, t_ref, x_ref, t_out, x_out, send_ref)


def merge(got_ref, t_ref, x_ref, t_out, x_out, send_ref):
    got_fades = got_ref[pl.ds(FADE, 16)].astype(F32)
    row = lax.broadcasted_iota(jnp.int32, (8, DIM), 0)
    fades, marks_t, marks_x = (jnp.zeros((8, DIM), F32) for _ in range(3))
    for h in range(2):
        rows = pl.ds(h * DIM, DIM)
        got = got_ref[rows].astype(F32)
        got_fade = got_fades[2 * h : 2 * h + 1] + got_fades[2 * h + 1 : 2 * h + 2]
        mine = t_ref[pl.ds(FADE, 8)][h : h + 1]
        state = mine * got + t_ref[rows]
        t_out[rows] = state
        send_ref[rows] = state.astype(BF16)
        fade = mine * got_fade
        if x_ref is None:
            x_out[rows] = got
            x_fade = got_fade
        else:
            before = x_ref[pl.ds(FADE, 8)][h : h + 1]
            x_out[rows] = before * got + x_ref[rows]
            x_fade = before * got_fade
        high = fade.astype(BF16).astype(F32)
        marks_t = jnp.where(row == h, fade, marks_t)
        marks_x = jnp.where(row == h, x_fade, marks_x)
        fades = jnp.where(row == 2 * h, high, jnp.where(row == 2 * h + 1, fade - high, fades))
    t_out[pl.ds(FADE, 8)] = marks_t
    x_out[pl.ds(FADE, 8)] = marks_x
    send_ref[pl.ds(FADE, 16)] = jnp.concatenate([fades, jnp.zeros((8, DIM), F32)], axis=0).astype(BF16)


def local_kernel(x_ref, w_ref, r_ref, g_ref, codes_ref, rates_ref, skip_ref, base_ref, carry_ref):
    sums = code_sums(codes_ref)
    lower = lax.broadcasted_iota(jnp.int32, (BLOCK, BLOCK), 0) >= lax.broadcasted_iota(
        jnp.int32, (BLOCK, BLOCK), 1
    )
    for h in range(2):
        cols = pl.ds(h * DIM, DIM)
        rate, skip = rates_ref[h], skip_ref[h]
        state, before = None, None
        for b in range(2):
            rows = pl.ds(b * BLOCK, BLOCK)
            across, down = square(sums[b, h])
            x, w, r = x_ref[rows, cols], w_ref[rows, cols], r_ref[rows, cols]
            decay = jnp.exp(jnp.minimum(rate * (across - down), 0.0))
            scores = dot(r, w, 1, 1)
            mix = jnp.where(lower, scores * decay, 0.0).astype(BF16)
            y = dot(mix, x) + skip * x.astype(F32)
            if b == 0:
                last = down[BLOCK - 1 : BLOCK]
                tail = jnp.exp(rate * (down - last))
                state = dot((w.astype(F32) * tail).astype(BF16), x, 0, 0)
                before = last
                carry = jnp.exp(-rate * down)
            else:
                high, low = split(state)
                y = y + jnp.exp(-rate * down) * (dot(r, high) + dot(r, low))
                carry = jnp.exp(-rate * (down + before))
            gate = g_ref[rows, cols].astype(F32)
            silu = gate / (1.0 + jnp.exp(-gate))
            base_ref[rows, cols] = y * silu
            carry_ref[rows, cols] = carry * silu


def to_lanes(v):
    halves = v[:, :DIM] + v[:, DIM:]
    return [
        jnp.sum(jnp.transpose(halves[b * DIM : (b + 1) * DIM]), axis=0, keepdims=True)
        for b in range(2)
    ]


def carried_kernel(
    got_ref, x_ref, r_ref, base_ref, carry_ref, rows_ref, a_ref, gated_ref, send_ref
):
    parts = []
    for h in range(2):
        rows, cols = pl.ds(h * DIM, DIM), pl.ds(h * DIM, DIM)
        before = x_ref[pl.ds(FADE, 8)][h : h + 1]
        entering = before * got_ref[rows].astype(F32) + x_ref[rows]
        high, low = split(entering)
        r = r_ref[:, cols]
        parts.append(base_ref[:, cols] + carry_ref[:, cols] * (dot(r, high) + dot(r, low)))
    gated = jnp.concatenate(parts, axis=1)
    gated_ref[...] = gated
    weight = rows_ref[1:2, :]
    stats = to_lanes(gated * gated) + to_lanes(gated * weight)
    stats = jnp.concatenate(stats + [a_ref[...], jnp.zeros((2, DIM), F32)], axis=0)
    for n in range(send_ref.shape[0]):
        send_ref[n] = stats


def keys_of(ref, k):
    return jnp.concatenate([ref[n, k + i, 0:64] for i in range(2) for n in range(4)], axis=0)


def values_of(ref, k):
    return jnp.concatenate([ref[n, k + i, 64:128] for i in range(2) for n in range(4)], axis=0)


def spread(q_ref, scaled_ref):
    c = math.log2(math.e) / math.sqrt(DIM)
    for h in range(2):
        high, low = split(q_ref[:, h * DIM : (h + 1) * DIM].astype(F32) * c)
        scaled_ref[pl.ds(h * 256, 256)] = jnp.concatenate([high, low], axis=1)


def scan_keys(kv_ref, core, scaled_ref, scores_ref, m_ref, l_ref, acc_ref, fresh):
    zl, here = lax.axis_index("zl"), lax.axis_index("core")
    tiles = zl + 1 if fresh else zl + here
    pairs = zl // 2 if fresh else tiles // 2
    rows = scaled_ref.shape[0]

    def lanes_max(s):
        return jnp.maximum(
            jnp.maximum(s[:, 0:128], s[:, 128:256]), jnp.maximum(s[:, 256:384], s[:, 384:512])
        )

    def scores(i):
        keys = keys_of(kv_ref, 2 * i)
        return dot(scaled_ref[...], jnp.concatenate([keys, keys], axis=1), 1, 1)

    def first(i, _):
        s = scores(i)
        scores_ref[i] = s
        m_ref[...] = jnp.maximum(m_ref[...], lanes_max(s))
        return 0

    def tail(i):
        key = lax.broadcasted_iota(jnp.int32, (rows, 512), 1)
        key = (i * 2) * 512 + core * 256 + jnp.where(key < 256, key, key + 256)
        spot = lax.broadcasted_iota(jnp.int32, (rows, 512), 0)
        spot = zl * 512 + here * 256 + jnp.where(spot < 256, spot, spot - 256)
        s = jnp.where(key <= spot, scores(i), NEG)
        scores_ref[i] = s
        m_ref[...] = jnp.maximum(m_ref[...], lanes_max(s))

    old = m_ref[...]
    lax.fori_loop(0, pairs, first, 0)
    ragged = 2 * pairs < tiles

    @pl.when(ragged)
    def _():
        tail(pairs)

    top = jnp.broadcast_to(jnp.max(m_ref[...], axis=1, keepdims=True), m_ref.shape)
    if fresh:
        l_ref[...] = jnp.zeros(l_ref.shape, F32)
        acc_ref[...] = jnp.zeros(acc_ref.shape, F32)
    else:
        fade = jnp.exp2(old - top)
        l_ref[...] = l_ref[...] * fade
        acc_ref[...] = acc_ref[...] * fade
    m_ref[...] = top

    def second(i, _):
        top = m_ref[...]
        p = [jnp.exp2(scores_ref[i, :, n : n + 128] - top) for n in range(0, 512, 128)]
        l_ref[...] += (p[0] + p[1]) + (p[2] + p[3])
        weights = jnp.concatenate([v.astype(BF16) for v in p], axis=1)
        acc_ref[...] += dot(weights, values_of(kv_ref, 2 * i))
        return 0

    lax.fori_loop(0, pairs + ragged.astype(jnp.int32), second, 0)


def attend_own_kernel(q_ref, kv_ref, scaled_ref, m_ref, l_ref, acc_ref, scores_ref):
    spread(q_ref, scaled_ref)
    m_ref[...] = jnp.full(m_ref.shape, NEG, F32)
    scan_keys(kv_ref, lax.axis_index("core"), scaled_ref, scores_ref, m_ref, l_ref, acc_ref, True)


def attend_other_kernel(
    scaled_ref, kv_ref, m_in, l_in, acc_in, rows_ref, o_ref, a_ref, m_ref, l_ref, acc_ref, scores_ref
):
    m_ref[...] = m_in[...]
    l_ref[...] = l_in[...]
    acc_ref[...] = acc_in[...]
    other = 1 - lax.axis_index("core")
    scan_keys(kv_ref, other, scaled_ref, scores_ref, m_ref, l_ref, acc_ref, False)
    parts = []
    for h in range(2):
        at = pl.ds(h * 256, 256)
        parts.append(acc_ref[at] / jnp.sum(l_ref[at], axis=1, keepdims=True))
    attended = jnp.concatenate(parts, axis=1).astype(BF16)
    o_ref[...] = attended
    a_ref[...] = jnp.concatenate(to_lanes(attended.astype(F32) * rows_ref[2:3, :]), axis=0)


def segment_row(values):
    full = jnp.concatenate([values, jnp.zeros((DIM - SEGMENTS, DIM), F32)], axis=0)
    return jnp.sum(jnp.transpose(full), axis=0, keepdims=True)


def middle_sums_kernel(got_ref, seg_ref, send_ref):
    total = got_ref[0]
    for n in range(1, got_ref.shape[0]):
        total = total + got_ref[n]
    segment = lax.broadcasted_iota(jnp.int32, (SEGMENTS, DIM), 0)
    seg = seg_ref[...]
    part = jnp.zeros((SEGMENTS, DIM), F32)
    for j in range(2):
        part = part + jnp.where(seg[j : j + 1] == segment, total[4 + j : 5 + j], 0.0)
    part = segment_row(part)
    high = part.astype(BF16).astype(F32)
    out = jnp.concatenate([total[0:4], high, part - high, seg.astype(F32)], axis=0).astype(BF16)
    for n in range(send_ref.shape[0]):
        send_ref[n] = out


def final_kernel(got_ref, gated_ref, rows_ref, o_ref, values_ref):
    index = lax.axis_index("zl") * 2 + lax.axis_index("core")
    mine = got_ref[2 * index].astype(F32) + got_ref[2 * index + 1].astype(F32)
    gain = rows_ref[0:1, :]
    for b in range(2):
        rows = pl.ds(b * DIM, DIM)
        scale = lax.rsqrt(mine[b : b + 1] * (1.0 / COLUMNS) + EPS)
        _, down = square(scale)
        for h in range(2):
            cols = slice(h * DIM, (h + 1) * DIM)
            o_ref[rows, cols] = (gated_ref[rows, cols] * down * gain[:, cols]).astype(BF16)
    segment = lax.broadcasted_iota(jnp.int32, (SEGMENTS, DIM), 0)
    part = jnp.zeros((SEGMENTS, DIM), F32)
    count = jnp.zeros((SEGMENTS, DIM), F32)
    extra = jnp.zeros((8, DIM), F32)
    for s in range(got_ref.shape[0] // 2):
        low = got_ref[2 * s].astype(F32)
        both = low + got_ref[2 * s + 1].astype(F32)
        extra = extra + both
        scale = lax.rsqrt(both[0:2] * (1.0 / COLUMNS) + EPS)
        score = scale * both[2:4]
        seg = low[6:8].astype(jnp.int32)
        for j in range(2):
            member = seg[j : j + 1] == segment
            part = part + jnp.where(member, score[j : j + 1], 0.0)
            count = count + jnp.where(member, 1.0, 0.0)
    total = segment_row(part) + extra[4:5] + extra[5:6]
    held = segment_row(count)
    values_ref[...] = (total / jnp.maximum(held, 1.0))[:, :SEGMENTS]


def per_device(
    queries,
    key_rows,
    value_rows,
    state_input,
    state_write,
    state_read,
    gate_input,
    decay_codes,
    decay_rates,
    skip_gain,
    norm_gain,
    attend_readout,
    state_readout,
    segment_index,
):
    tokens = queries.shape[0]
    codes = decay_codes.T
    seg = segment_index.reshape(2, DIM)
    gain = norm_gain.reshape(1, 256)
    state_out = state_readout.reshape(1, 256)
    attend_out = attend_readout.reshape(1, 256)
    chips, wide = lax.axis_size("zl"), lax.axis_size("x")
    ctx = chips * lax.axis_size("core")

    together = lax.optimization_barrier
    own, send, packed, rows, seg = call(
        entry_kernel,
        (
            shape((FADE + 8, DIM)),
            shape((STATE_ROWS, DIM), BF16),
            shape((chips, DIM, DIM), BF16),
            shape((8, 256)),
            shape((2, DIM), jnp.int32),
        ),
        [VMEM] * 3 + [SMEM] + [HBM] * 2 + [VMEM] * 4,
        [pltpu.VMEM((DIM, DIM), BF16), pltpu.SemaphoreType.DMA((2,))],
        mib=53,
    )(
        state_input, state_write, codes, decay_rates, key_rows, value_rows, gain, state_out, attend_out, seg
    )

    def shifted(v, by):
        return lax.ppermute(v, CTX, [(i, i + by) for i in range(ctx - by)])

    merged = (shape((FADE + 8, DIM)), shape((FADE + 8, DIM)), shape((STATE_ROWS, DIM), BF16))
    got = shifted(send, 1)
    quarter = lax.all_to_all(packed, "zl", 0, 0)
    t, before, send = call(first_kernel, merged, [VMEM] * 2)(got, own)
    got = shifted(send, 2)
    got, quarter = together((got, quarter))
    fan_shape = shape((wide, chips, DIM, DIM), BF16)
    t, before, send, fan = call(fan_kernel, merged + (fan_shape,), [VMEM] * 4)(got, t, before, quarter)

    mine = lax.all_to_all(fan, "x", 0, 0)
    got = shifted(send, 4)
    t, before, send = call(middle_kernel, merged, [VMEM] * 3)(got, t, before)
    base, carry = call(
        local_kernel, (shape((tokens, 256)), shape((tokens, 256))), [VMEM] * 5 + [SMEM] * 2
    )(state_input, state_write, state_read, gate_input, codes, decay_rates, skip_gain)
    send, base, mine = together((send, base, mine))

    got = shifted(send, 8)
    theirs = lax.ppermute(mine, "core", [(0, 1), (1, 0)])
    running = (shape((512, 256), BF16),) + (shape((512, DIM)),) * 3
    scores = pltpu.VMEM((chips // 2, 512, 512), F32)
    attention = call(attend_own_kernel, running, [VMEM] * 2, [scores], flops=10**9)(queries, mine)
    theirs, attention = together((theirs, attention))
    attended, a = call(
        attend_other_kernel,
        (shape((tokens, 256), BF16), shape((2, DIM))),
        [VMEM] * 6,
        [pltpu.VMEM((512, DIM), F32) for _ in range(3)] + [scores],
        flops=10**9,
    )(attention[0], theirs, *attention[1:], rows)
    got, a = together((got, a))
    head_plane = lax.axis_size("y") * wide
    gated, send = call(
        carried_kernel, (shape((tokens, 256)), shape((head_plane, 8, DIM))), [VMEM] * 7
    )(got, before, state_read, base, carry, rows, a)
    summed = lax.all_to_all(send, ("y", "x"), 0, 0)
    line = ctx * lax.axis_size("zh")
    send = call(middle_sums_kernel, shape((line, 8, DIM), BF16), [VMEM] * 2)(summed, seg)
    summed = lax.all_to_all(send, ("zl", "core", "zh"), 0, 0)
    state_mixed, values = call(
        final_kernel, (shape((tokens, 256), BF16), shape((1, SEGMENTS))), [VMEM] * 3
    )(summed, gated, rows)
    return attended, state_mixed, values.reshape(SEGMENTS)


def solution(mesh):
    grid = mesh.devices.shape
    inner = Mesh(mesh.devices.reshape(grid[0] // 2, 2, 2, 4, grid[1] // 8), CTX + HEAD)
    both = P(CTX, HEAD)
    rows, heads = P(CTX), P(HEAD)
    in_specs = (both, P(CTX, None), P(CTX, None)) + (both,) * 5 + (heads,) * 5 + (rows,)
    return jax.shard_map(
        per_device, mesh=inner, in_specs=in_specs, out_specs=(both, both, P()), check_vma=False
    )
```

```python
import functools
import math

import jax
import jax.numpy as jnp
from jax import lax
from jax.experimental import pallas as pl
from jax.experimental.pallas import tpu as pltpu
from jax.sharding import Mesh
from jax.sharding import PartitionSpec as P

HEADS = 64
KV_HEADS = 8
DIM = 128
BLOCK = 128
SEGMENTS = 32
COLUMNS = 8192
EPS = 1e-5

F32 = jnp.float32
BF16 = jnp.bfloat16
CTX = ("zl", "core")
HEAD = ("zh", "y", "x")
VMEM = pl.BlockSpec(memory_space=pltpu.VMEM)
SMEM = pl.BlockSpec(memory_space=pltpu.SMEM)
HBM = pl.BlockSpec(memory_space=pltpu.HBM)
NEG = -1e30
CARRIED_FLOPS = 10_800_000_000
ENTRY_MIB = 58
FADE = 2 * DIM
STATE_ROWS = FADE + 16


def call(kernel, outs, ins, scratch=(), flops=10**6, moved=10**6, mib=24):
    many = isinstance(outs, (tuple, list))
    return pl.pallas_call(
        kernel,
        out_shape=outs,
        in_specs=ins,
        out_specs=[VMEM] * len(outs) if many else VMEM,
        scratch_shapes=scratch,
        cost_estimate=pl.CostEstimate(flops=flops, bytes_accessed=moved, transcendentals=0),
        compiler_params=pltpu.CompilerParams(vmem_limit_bytes=int(mib * 2**20)),
    )


def shape(dims, kind=F32):
    return jax.ShapeDtypeStruct(dims, kind)


def dot(a, b, ca=1, cb=0):
    return lax.dot_general(a, b, (((ca,), (cb,)), ((), ())), preferred_element_type=F32)


def split(v):
    high = v.astype(BF16)
    return high, (v - high.astype(F32)).astype(BF16)


def code_sums(codes_ref):
    rows = []
    for b in range(2):
        part = codes_ref[:, b * BLOCK : (b + 1) * BLOCK]
        rows += [part >> 6, part & 63]
    stacked = jnp.concatenate(rows, axis=0).astype(F32).astype(BF16)
    upto = lax.broadcasted_iota(jnp.int32, (BLOCK, BLOCK), 0) <= lax.broadcasted_iota(
        jnp.int32, (BLOCK, BLOCK), 1
    )
    total = dot(stacked, jnp.where(upto, 1.0, 0.0).astype(BF16))
    sums = {}
    for b in range(2):
        for h in range(2):
            sums[b, h] = 64.0 * total[4 * b + h : 4 * b + h + 1] + total[4 * b + 2 + h : 4 * b + 3 + h]
    return sums


def square(row):
    lanes = jnp.broadcast_to(row, (DIM, DIM))
    return lanes, jnp.transpose(lanes)


def entry_kernel(
    rates_ref, k_hbm, v_hbm, x_hbm, w_hbm, codes_hbm, gain_hbm, state_out_hbm, attend_out_hbm, seg_hbm,
    own_ref, send_ref, packed_ref, rows_ref,
    piece, x_ref, w_ref, codes_ref, gain_ref, state_out_ref, attend_out_ref, seg_ref, sems,
):
    group = lax.axis_index("zh") * 4 + lax.axis_index("y")
    quarter = pl.ds(pl.multiple_of(lax.axis_index("x") * 64, 64), 64)
    columns = pl.ds(pl.multiple_of(group * DIM, DIM), DIM)
    pairs = [(codes_hbm, codes_ref), (x_hbm, x_ref), (w_hbm, w_ref)]
    pairs += [(ref.at[quarter, columns], piece.at[pl.ds(64 * n, 64)]) for n, ref in enumerate((k_hbm, v_hbm))]
    pairs += [
        (gain_hbm, gain_ref),
        (state_out_hbm, state_out_ref),
        (attend_out_hbm, attend_out_ref),
        (seg_hbm, seg_ref),
    ]
    copies = [pltpu.make_async_copy(*pair, sems.at[n]) for n, pair in enumerate(pairs)]
    for c in copies:
        c.start()
    for c in copies[:3]:
        c.wait()
    sums = code_sums(codes_ref)
    row = lax.broadcasted_iota(jnp.int32, (8, DIM), 0)
    fades, marks = jnp.zeros((8, DIM), F32), jnp.zeros((8, DIM), F32)
    for h in range(2):
        cols = pl.ds(h * DIM, DIM)
        rate = rates_ref[h]
        state = None
        whole = None
        for b in range(2):
            rows = pl.ds(b * BLOCK, BLOCK)
            _, down = square(sums[b, h])
            last = down[BLOCK - 1 : BLOCK]
            tail = jnp.exp(rate * (down - last))
            written = (w_ref[rows, cols].astype(F32) * tail).astype(BF16)
            added = dot(written, x_ref[rows, cols], 0, 0)
            fade = jnp.exp(-rate * last)
            state = added if b == 0 else fade * state + added
            whole = last if b == 0 else whole + last
        own_ref[pl.ds(h * DIM, DIM)] = state
        send_ref[pl.ds(h * DIM, DIM)] = state.astype(BF16)
        fade = jnp.exp(-rate * whole)
        high = fade.astype(BF16).astype(F32)
        marks = jnp.where(row == h, fade, marks)
        fades = jnp.where(row == 2 * h, high, jnp.where(row == 2 * h + 1, fade - high, fades))
    own_ref[pl.ds(FADE, 8)] = marks
    send_ref[pl.ds(FADE, 16)] = jnp.concatenate([fades, jnp.zeros((8, DIM), F32)], axis=0).astype(BF16)
    for c in copies[3:]:
        c.wait()
    both = piece[...]
    for n in range(packed_ref.shape[0]):
        packed_ref[n] = both
    gain = gain_ref[...]
    rows_ref[...] = jnp.concatenate(
        [gain, gain * state_out_ref[...], attend_out_ref[...], seg_ref[...].astype(F32), jnp.zeros((4, 256), F32)],
        axis=0,
    )


def fan_kernel(
    got1_ref, got2_ref, got3_ref, own_ref, quarter_ref, rows_ref, x_out, send_ref, fan_ref, rows_out
):
    rows_out[...] = rows_ref[...]
    for n in range(fan_ref.shape[0]):
        fan_ref[n] = quarter_ref[...]
    refs = (got1_ref, got2_ref, got3_ref)
    sent = [ref[pl.ds(FADE, 16)].astype(F32) for ref in refs]
    row = lax.broadcasted_iota(jnp.int32, (8, DIM), 0)
    fades, marks = jnp.zeros((8, DIM), F32), jnp.zeros((8, DIM), F32)
    for h in range(2):
        rows = pl.ds(h * DIM, DIM)
        f1, f2, f3 = (v[2 * h : 2 * h + 1] + v[2 * h + 1 : 2 * h + 2] for v in sent)
        g1, g2, g3 = (ref[rows].astype(F32) for ref in refs)
        before = g1 + f1 * (g2 + f2 * g3)
        x_out[rows] = before
        own = own_ref[pl.ds(FADE, 8)][h : h + 1]
        send_ref[rows] = (own * before + own_ref[rows]).astype(BF16)
        past = f1 * f2 * f3
        marks = jnp.where(row == h, past, marks)
        fade = own * past
        high = fade.astype(BF16).astype(F32)
        fades = jnp.where(row == 2 * h, high, jnp.where(row == 2 * h + 1, fade - high, fades))
    x_out[pl.ds(FADE, 8)] = marks
    send_ref[pl.ds(FADE, 16)] = jnp.concatenate([fades, jnp.zeros((8, DIM), F32)], axis=0).astype(BF16)


def local_kernel(x_ref, w_ref, r_ref, g_ref, codes_ref, rates_ref, skip_ref, base_ref, carry_ref):
    sums = code_sums(codes_ref)
    lower = lax.broadcasted_iota(jnp.int32, (BLOCK, BLOCK), 0) >= lax.broadcasted_iota(
        jnp.int32, (BLOCK, BLOCK), 1
    )
    for h in range(2):
        cols = pl.ds(h * DIM, DIM)
        rate, skip = rates_ref[h], skip_ref[h]
        state, before = None, None
        for b in range(2):
            rows = pl.ds(b * BLOCK, BLOCK)
            across, down = square(sums[b, h])
            x, w, r = x_ref[rows, cols], w_ref[rows, cols], r_ref[rows, cols]
            decay = jnp.exp(jnp.minimum(rate * (across - down), 0.0))
            scores = dot(r, w, 1, 1)
            mix = jnp.where(lower, scores * decay, 0.0).astype(BF16)
            y = dot(mix, x) + skip * x.astype(F32)
            if b == 0:
                last = down[BLOCK - 1 : BLOCK]
                tail = jnp.exp(rate * (down - last))
                state = dot((w.astype(F32) * tail).astype(BF16), x, 0, 0)
                before = last
                carry = jnp.exp(-rate * down)
            else:
                high, low = split(state)
                y = y + jnp.exp(-rate * down) * (dot(r, high) + dot(r, low))
                carry = jnp.exp(-rate * (down + before))
            gate = g_ref[rows, cols].astype(F32)
            silu = gate / (1.0 + jnp.exp(-gate))
            base_ref[rows, cols] = y * silu
            carry_ref[rows, cols] = carry * silu


def to_lanes(v):
    halves = v[:, :DIM] + v[:, DIM:]
    return [
        jnp.sum(jnp.transpose(halves[b * DIM : (b + 1) * DIM]), axis=0, keepdims=True)
        for b in range(2)
    ]


def carried_kernel(
    near_ref, mid_ref, far_ref, x_ref, r_ref, base_ref, carry_ref, rows_ref, gated_ref, stats_ref
):
    parts = []
    near, mid = near_ref[pl.ds(FADE, 16)].astype(F32), mid_ref[pl.ds(FADE, 16)].astype(F32)
    for h in range(2):
        rows, cols = pl.ds(h * DIM, DIM), pl.ds(h * DIM, DIM)
        entering = far_ref[rows].astype(F32)
        for ref, fades in ((mid_ref, mid), (near_ref, near)):
            fade = fades[2 * h : 2 * h + 1] + fades[2 * h + 1 : 2 * h + 2]
            entering = fade * entering + ref[rows].astype(F32)
        entering = x_ref[pl.ds(FADE, 8)][h : h + 1] * entering + x_ref[rows]
        high, low = split(entering)
        r = r_ref[:, cols]
        parts.append(base_ref[:, cols] + carry_ref[:, cols] * (dot(r, high) + dot(r, low)))
    gated = jnp.concatenate(parts, axis=1)
    gated_ref[...] = gated
    weight = rows_ref[1:2, :]
    stats_ref[...] = jnp.concatenate(to_lanes(gated * gated) + to_lanes(gated * weight), axis=0)


def keys_of(ref, k):
    return jnp.concatenate([ref[n, k + i, 0:64] for i in range(2) for n in range(4)], axis=0)


def values_of(ref, k):
    return jnp.concatenate([ref[n, k + i, 64:128] for i in range(2) for n in range(4)], axis=0)


def spread(q_ref, scaled_ref):
    c = math.log2(math.e) / math.sqrt(DIM)
    for h in range(2):
        high, low = split(q_ref[:, h * DIM : (h + 1) * DIM].astype(F32) * c)
        scaled_ref[pl.ds(h * 256, 256)] = jnp.concatenate([high, low], axis=1)


def scan_keys(kv_ref, core, scaled_ref, scores_ref, m_ref, l_ref, acc_ref, fresh):
    zl, here = lax.axis_index("zl"), lax.axis_index("core")
    tiles = zl + 1 if fresh else zl + here
    pairs = zl // 2 if fresh else tiles // 2
    rows = scaled_ref.shape[0]

    def lanes_max(s):
        return jnp.maximum(
            jnp.maximum(s[:, 0:128], s[:, 128:256]), jnp.maximum(s[:, 256:384], s[:, 384:512])
        )

    def scores(i):
        keys = keys_of(kv_ref, 2 * i)
        return dot(scaled_ref[...], jnp.concatenate([keys, keys], axis=1), 1, 1)

    def first(i, _):
        s = scores(i)
        scores_ref[i] = s
        m_ref[...] = jnp.maximum(m_ref[...], lanes_max(s))
        return 0

    def tail(i):
        key = lax.broadcasted_iota(jnp.int32, (rows, 512), 1)
        key = (i * 2) * 512 + core * 256 + jnp.where(key < 256, key, key + 256)
        spot = lax.broadcasted_iota(jnp.int32, (rows, 512), 0)
        spot = zl * 512 + here * 256 + jnp.where(spot < 256, spot, spot - 256)
        s = jnp.where(key <= spot, scores(i), NEG)
        scores_ref[i] = s
        m_ref[...] = jnp.maximum(m_ref[...], lanes_max(s))

    old = m_ref[...]
    lax.fori_loop(0, pairs, first, 0)
    ragged = 2 * pairs < tiles

    @pl.when(ragged)
    def _():
        tail(pairs)

    top = jnp.broadcast_to(jnp.max(m_ref[...], axis=1, keepdims=True), m_ref.shape)
    if fresh:
        l_ref[...] = jnp.zeros(l_ref.shape, F32)
        acc_ref[...] = jnp.zeros(acc_ref.shape, F32)
    else:
        fade = jnp.exp2(old - top)
        l_ref[...] = l_ref[...] * fade
        acc_ref[...] = acc_ref[...] * fade
    m_ref[...] = top

    def second(i, _):
        top = m_ref[...]
        p = [jnp.exp2(scores_ref[i, :, n : n + 128] - top) for n in range(0, 512, 128)]
        l_ref[...] += (p[0] + p[1]) + (p[2] + p[3])
        weights = jnp.concatenate([v.astype(BF16) for v in p], axis=1)
        acc_ref[...] += dot(weights, values_of(kv_ref, 2 * i))
        return 0

    lax.fori_loop(0, pairs + ragged.astype(jnp.int32), second, 0)


def attend_own_kernel(q_ref, kv_ref, scaled_ref, m_ref, l_ref, acc_ref, scores_ref):
    spread(q_ref, scaled_ref)
    m_ref[...] = jnp.full(m_ref.shape, NEG, F32)
    scan_keys(kv_ref, lax.axis_index("core"), scaled_ref, scores_ref, m_ref, l_ref, acc_ref, True)


def attend_other_kernel(
    scaled_ref, kv_ref, m_in, l_in, acc_in, rows_ref, stats_ref,
    o_ref, send_ref, m_ref, l_ref, acc_ref, scores_ref,
):
    m_ref[...] = m_in[...]
    l_ref[...] = l_in[...]
    acc_ref[...] = acc_in[...]
    other = 1 - lax.axis_index("core")
    scan_keys(kv_ref, other, scaled_ref, scores_ref, m_ref, l_ref, acc_ref, False)
    parts = []
    for h in range(2):
        at = pl.ds(h * 256, 256)
        parts.append(acc_ref[at] / jnp.sum(l_ref[at], axis=1, keepdims=True))
    attended = jnp.concatenate(parts, axis=1).astype(BF16)
    o_ref[...] = attended
    a = to_lanes(attended.astype(F32) * rows_ref[2:3, :])
    stats = jnp.concatenate([stats_ref[...]] + a + [jnp.zeros((2, DIM), F32)], axis=0)
    for n in range(send_ref.shape[0]):
        send_ref[n] = stats


def segment_row(values):
    full = jnp.concatenate([values, jnp.zeros((DIM - SEGMENTS, DIM), F32)], axis=0)
    return jnp.sum(jnp.transpose(full), axis=0, keepdims=True)


def middle_sums_kernel(got_ref, rows_ref, send_ref):
    total = got_ref[0]
    for n in range(1, got_ref.shape[0]):
        total = total + got_ref[n]
    segment = lax.broadcasted_iota(jnp.int32, (SEGMENTS, DIM), 0)
    seg = jnp.concatenate([rows_ref[3:4, :DIM], rows_ref[3:4, DIM:]], axis=0)
    held = seg.astype(jnp.int32)
    part = jnp.zeros((SEGMENTS, DIM), F32)
    for j in range(2):
        part = part + jnp.where(held[j : j + 1] == segment, total[4 + j : 5 + j], 0.0)
    part = segment_row(part)
    high = part.astype(BF16).astype(F32)
    out = jnp.concatenate([total[0:4], high, part - high, seg], axis=0).astype(BF16)
    for n in range(send_ref.shape[0]):
        send_ref[n] = out


def final_kernel(got_ref, gated_ref, rows_ref, o_ref, values_ref):
    index = lax.axis_index("zl") * 2 + lax.axis_index("core")
    mine = got_ref[2 * index].astype(F32) + got_ref[2 * index + 1].astype(F32)
    gain = rows_ref[0:1, :]
    for b in range(2):
        rows = pl.ds(b * DIM, DIM)
        scale = lax.rsqrt(mine[b : b + 1] * (1.0 / COLUMNS) + EPS)
        _, down = square(scale)
        for h in range(2):
            cols = slice(h * DIM, (h + 1) * DIM)
            o_ref[rows, cols] = (gated_ref[rows, cols] * down * gain[:, cols]).astype(BF16)
    segment = lax.broadcasted_iota(jnp.int32, (SEGMENTS, DIM), 0)
    part = jnp.zeros((SEGMENTS, DIM), F32)
    count = jnp.zeros((SEGMENTS, DIM), F32)
    extra = jnp.zeros((8, DIM), F32)
    for s in range(got_ref.shape[0] // 2):
        low = got_ref[2 * s].astype(F32)
        both = low + got_ref[2 * s + 1].astype(F32)
        extra = extra + both
        scale = lax.rsqrt(both[0:2] * (1.0 / COLUMNS) + EPS)
        score = scale * both[2:4]
        seg = low[6:8].astype(jnp.int32)
        for j in range(2):
            member = seg[j : j + 1] == segment
            part = part + jnp.where(member, score[j : j + 1], 0.0)
            count = count + jnp.where(member, 1.0, 0.0)
    total = segment_row(part) + extra[4:5] + extra[5:6]
    held = segment_row(count)
    values_ref[...] = (total / jnp.maximum(held, 1.0))[:, :SEGMENTS]


def per_device(
    queries,
    key_rows,
    value_rows,
    state_input,
    state_write,
    state_read,
    gate_input,
    decay_codes,
    decay_rates,
    skip_gain,
    norm_gain,
    attend_readout,
    state_readout,
    segment_index,
):
    tokens = queries.shape[0]
    codes = decay_codes.T
    seg = segment_index.reshape(1, 256)
    gain = norm_gain.reshape(1, 256)
    state_out = state_readout.reshape(1, 256)
    attend_out = attend_readout.reshape(1, 256)
    chips, wide = lax.axis_size("zl"), lax.axis_size("x")
    ctx = chips * lax.axis_size("core")

    together = lax.optimization_barrier
    own, send, packed, rows = call(
        entry_kernel,
        (
            shape((FADE + 8, DIM)),
            shape((STATE_ROWS, DIM), BF16),
            shape((chips, DIM, DIM), BF16),
            shape((8, 256)),
        ),
        [SMEM] + [HBM] * 9,
        [
            pltpu.VMEM((DIM, DIM), BF16),
            pltpu.VMEM((tokens, 256), BF16),
            pltpu.VMEM((tokens, 256), BF16),
            pltpu.VMEM((2, tokens), jnp.int32),
            pltpu.VMEM((1, 256), F32),
            pltpu.VMEM((1, 256), F32),
            pltpu.VMEM((1, 256), F32),
            pltpu.VMEM((1, 256), jnp.int32),
            pltpu.SemaphoreType.DMA((9,)),
        ],
        mib=ENTRY_MIB,
    )(decay_rates, key_rows, value_rows, state_input, state_write, codes, gain, state_out, attend_out, seg)

    def shifted(v, by):
        return lax.ppermute(v, CTX, [(i, i + by) for i in range(ctx - by)])

    quarter = lax.all_to_all(packed, "zl", 0, 0)
    got = tuple(shifted(send, by) for by in (3, 2, 1))
    base, carry = call(
        local_kernel, (shape((tokens, 256)), shape((tokens, 256))), [VMEM] * 5 + [SMEM] * 2
    )(state_input, state_write, state_read, gate_input, codes, decay_rates, skip_gain)
    got, quarter, base = together((got, quarter, base))
    before, send, fan, rows = call(
        fan_kernel,
        (
            shape((FADE + 8, DIM)),
            shape((STATE_ROWS, DIM), BF16),
            shape((wide, chips, DIM, DIM), BF16),
            shape((8, 256)),
        ),
        [VMEM] * 6,
    )(*got[::-1], own, quarter, rows)

    mine = lax.all_to_all(fan, "x", 0, 0)
    arrived = tuple(shifted(send, by) for by in (4, 8, 12))
    theirs = lax.ppermute(mine, "core", [(0, 1), (1, 0)])
    running = (shape((512, 256), BF16),) + (shape((512, DIM)),) * 3
    scores = pltpu.VMEM((chips // 2, 512, 512), F32)
    attention = call(attend_own_kernel, running, [VMEM] * 2, [scores], flops=10**9)(queries, mine)
    arrived, attention = together((arrived, attention))
    near, mid, far = arrived
    gated, stats = call(
        carried_kernel, (shape((tokens, 256)), shape((4, DIM))), [VMEM] * 8, flops=CARRIED_FLOPS
    )(near, mid, far, before, state_read, base, carry, rows)
    theirs, attention, stats = together((theirs, attention, stats))
    head_plane = lax.axis_size("y") * wide
    attended, send = call(
        attend_other_kernel,
        (shape((tokens, 256), BF16), shape((head_plane, 8, DIM))),
        [VMEM] * 7,
        [pltpu.VMEM((512, DIM), F32) for _ in range(3)] + [scores],
        flops=10**9,
    )(attention[0], theirs, *attention[1:], rows, stats)
    summed = lax.all_to_all(send, ("y", "x"), 0, 0)
    line = ctx * lax.axis_size("zh")
    send = call(middle_sums_kernel, shape((line, 8, DIM), BF16), [VMEM] * 2)(summed, rows)
    summed = lax.all_to_all(send, ("zl", "core", "zh"), 0, 0)
    state_mixed, values = call(
        final_kernel, (shape((tokens, 256), BF16), shape((1, SEGMENTS))), [VMEM] * 3
    )(summed, gated, rows)
    return attended, state_mixed, values.reshape(SEGMENTS)


def solution(mesh):
    grid = mesh.devices.shape
    inner = Mesh(mesh.devices.reshape(grid[0] // 2, 2, 2, 4, grid[1] // 8), CTX + HEAD)
    both = P(CTX, HEAD)
    rows, heads = P(CTX), P(HEAD)
    in_specs = (both, P(CTX, None), P(CTX, None)) + (both,) * 5 + (heads,) * 5 + (rows,)
    return jax.shard_map(
        per_device, mesh=inner, in_specs=in_specs, out_specs=(both, both, P()), check_vma=False
    )
```

```python
import functools
import math

import jax
import jax.numpy as jnp
from jax import lax
from jax.experimental import pallas as pl
from jax.experimental.pallas import tpu as pltpu
from jax.sharding import Mesh
from jax.sharding import PartitionSpec as P

HEADS = 64
KV_HEADS = 8
DIM = 128
BLOCK = 128
SEGMENTS = 32
COLUMNS = 8192
EPS = 1e-5

F32 = jnp.float32
BF16 = jnp.bfloat16
CTX = ("zl", "core")
HEAD = ("zh", "y", "x")
VMEM = pl.BlockSpec(memory_space=pltpu.VMEM)
SMEM = pl.BlockSpec(memory_space=pltpu.SMEM)
HBM = pl.BlockSpec(memory_space=pltpu.HBM)
NEG = -1e30
CARRIED_FLOPS = 10_800_000_000
MERGE_FLOPS = 20_000_000_000
PACK_MIB = 58
FADE = 2 * DIM
STATE_ROWS = FADE + 16


def call(kernel, outs, ins, scratch=(), flops=10**6, moved=10**6, mib=24):
    many = isinstance(outs, (tuple, list))
    return pl.pallas_call(
        kernel,
        out_shape=outs,
        in_specs=ins,
        out_specs=[VMEM] * len(outs) if many else VMEM,
        scratch_shapes=scratch,
        cost_estimate=pl.CostEstimate(flops=flops, bytes_accessed=moved, transcendentals=0),
        compiler_params=pltpu.CompilerParams(vmem_limit_bytes=int(mib * 2**20)),
    )


def shape(dims, kind=F32):
    return jax.ShapeDtypeStruct(dims, kind)


def dot(a, b, ca=1, cb=0):
    return lax.dot_general(a, b, (((ca,), (cb,)), ((), ())), preferred_element_type=F32)


def split(v):
    high = v.astype(BF16)
    return high, (v - high.astype(F32)).astype(BF16)


def code_sums(codes_ref):
    rows = []
    for b in range(2):
        part = codes_ref[:, b * BLOCK : (b + 1) * BLOCK]
        rows += [part >> 6, part & 63]
    stacked = jnp.concatenate(rows, axis=0).astype(F32).astype(BF16)
    upto = lax.broadcasted_iota(jnp.int32, (BLOCK, BLOCK), 0) <= lax.broadcasted_iota(
        jnp.int32, (BLOCK, BLOCK), 1
    )
    total = dot(stacked, jnp.where(upto, 1.0, 0.0).astype(BF16))
    sums = {}
    for b in range(2):
        for h in range(2):
            sums[b, h] = 64.0 * total[4 * b + h : 4 * b + h + 1] + total[4 * b + 2 + h : 4 * b + 3 + h]
    return sums


def square(row):
    lanes = jnp.broadcast_to(row, (DIM, DIM))
    return lanes, jnp.transpose(lanes)


def pack_kernel(k_hbm, v_hbm, packed_ref, piece, sems):
    group = lax.axis_index("zh") * 4 + lax.axis_index("y")
    quarter = pl.ds(pl.multiple_of(lax.axis_index("x") * 64, 64), 64)
    columns = pl.ds(pl.multiple_of(group * DIM, DIM), DIM)
    copies = [
        pltpu.make_async_copy(ref.at[quarter, columns], piece.at[pl.ds(64 * n, 64)], sems.at[n])
        for n, ref in enumerate((k_hbm, v_hbm))
    ]
    for c in copies:
        c.start()
    for c in copies:
        c.wait()
    both = piece[...]
    for n in range(packed_ref.shape[0]):
        packed_ref[n] = both


def states_kernel(
    rates_ref, x_ref, w_ref, codes_ref, gain_ref, state_out_ref, attend_out_ref, seg_ref,
    own_ref, send_ref, rows_ref,
):
    sums = code_sums(codes_ref)
    row = lax.broadcasted_iota(jnp.int32, (8, DIM), 0)
    fades, marks = jnp.zeros((8, DIM), F32), jnp.zeros((8, DIM), F32)
    for h in range(2):
        cols = pl.ds(h * DIM, DIM)
        rate = rates_ref[h]
        state = None
        whole = None
        for b in range(2):
            rows = pl.ds(b * BLOCK, BLOCK)
            _, down = square(sums[b, h])
            last = down[BLOCK - 1 : BLOCK]
            tail = jnp.exp(rate * (down - last))
            written = (w_ref[rows, cols].astype(F32) * tail).astype(BF16)
            added = dot(written, x_ref[rows, cols], 0, 0)
            fade = jnp.exp(-rate * last)
            state = added if b == 0 else fade * state + added
            whole = last if b == 0 else whole + last
        own_ref[pl.ds(h * DIM, DIM)] = state
        send_ref[pl.ds(h * DIM, DIM)] = state.astype(BF16)
        fade = jnp.exp(-rate * whole)
        high = fade.astype(BF16).astype(F32)
        marks = jnp.where(row == h, fade, marks)
        fades = jnp.where(row == 2 * h, high, jnp.where(row == 2 * h + 1, fade - high, fades))
    own_ref[pl.ds(FADE, 8)] = marks
    send_ref[pl.ds(FADE, 16)] = jnp.concatenate([fades, jnp.zeros((8, DIM), F32)], axis=0).astype(BF16)
    gain = gain_ref[...]
    rows_ref[...] = jnp.concatenate(
        [gain, gain * state_out_ref[...], attend_out_ref[...], seg_ref[...].astype(F32), jnp.zeros((4, 256), F32)],
        axis=0,
    )


def fan_kernel(quarter_ref, fan_ref):
    for n in range(fan_ref.shape[0]):
        fan_ref[n] = quarter_ref[...]


def merge_kernel(got1_ref, got2_ref, got3_ref, own_ref, x_out, send_ref):
    refs = (got1_ref, got2_ref, got3_ref)
    sent = [ref[pl.ds(FADE, 16)].astype(F32) for ref in refs]
    row = lax.broadcasted_iota(jnp.int32, (8, DIM), 0)
    fades, marks = jnp.zeros((8, DIM), F32), jnp.zeros((8, DIM), F32)
    for h in range(2):
        rows = pl.ds(h * DIM, DIM)
        f1, f2, f3 = (v[2 * h : 2 * h + 1] + v[2 * h + 1 : 2 * h + 2] for v in sent)
        g1, g2, g3 = (ref[rows].astype(F32) for ref in refs)
        before = g1 + f1 * (g2 + f2 * g3)
        x_out[rows] = before
        own = own_ref[pl.ds(FADE, 8)][h : h + 1]
        send_ref[rows] = (own * before + own_ref[rows]).astype(BF16)
        past = f1 * f2 * f3
        marks = jnp.where(row == h, past, marks)
        fade = own * past
        high = fade.astype(BF16).astype(F32)
        fades = jnp.where(row == 2 * h, high, jnp.where(row == 2 * h + 1, fade - high, fades))
    x_out[pl.ds(FADE, 8)] = marks
    send_ref[pl.ds(FADE, 16)] = jnp.concatenate([fades, jnp.zeros((8, DIM), F32)], axis=0).astype(BF16)


def local_kernel(x_ref, w_ref, r_ref, g_ref, codes_ref, rates_ref, skip_ref, base_ref, carry_ref):
    sums = code_sums(codes_ref)
    lower = lax.broadcasted_iota(jnp.int32, (BLOCK, BLOCK), 0) >= lax.broadcasted_iota(
        jnp.int32, (BLOCK, BLOCK), 1
    )
    for h in range(2):
        cols = pl.ds(h * DIM, DIM)
        rate, skip = rates_ref[h], skip_ref[h]
        state, before = None, None
        for b in range(2):
            rows = pl.ds(b * BLOCK, BLOCK)
            across, down = square(sums[b, h])
            x, w, r = x_ref[rows, cols], w_ref[rows, cols], r_ref[rows, cols]
            decay = jnp.exp(jnp.minimum(rate * (across - down), 0.0))
            scores = dot(r, w, 1, 1)
            mix = jnp.where(lower, scores * decay, 0.0).astype(BF16)
            y = dot(mix, x) + skip * x.astype(F32)
            if b == 0:
                last = down[BLOCK - 1 : BLOCK]
                tail = jnp.exp(rate * (down - last))
                state = dot((w.astype(F32) * tail).astype(BF16), x, 0, 0)
                before = last
                carry = jnp.exp(-rate * down)
            else:
                high, low = split(state)
                y = y + jnp.exp(-rate * down) * (dot(r, high) + dot(r, low))
                carry = jnp.exp(-rate * (down + before))
            gate = g_ref[rows, cols].astype(F32)
            silu = gate / (1.0 + jnp.exp(-gate))
            base_ref[rows, cols] = y * silu
            carry_ref[rows, cols] = carry * silu


def to_lanes(v):
    halves = v[:, :DIM] + v[:, DIM:]
    return [
        jnp.sum(jnp.transpose(halves[b * DIM : (b + 1) * DIM]), axis=0, keepdims=True)
        for b in range(2)
    ]


def carried_kernel(
    near_ref, mid_ref, far_ref, x_ref, r_ref, base_ref, carry_ref, rows_ref, gated_ref, stats_ref
):
    parts = []
    near, mid = near_ref[pl.ds(FADE, 16)].astype(F32), mid_ref[pl.ds(FADE, 16)].astype(F32)
    for h in range(2):
        rows, cols = pl.ds(h * DIM, DIM), pl.ds(h * DIM, DIM)
        entering = far_ref[rows].astype(F32)
        for ref, fades in ((mid_ref, mid), (near_ref, near)):
            fade = fades[2 * h : 2 * h + 1] + fades[2 * h + 1 : 2 * h + 2]
            entering = fade * entering + ref[rows].astype(F32)
        entering = x_ref[pl.ds(FADE, 8)][h : h + 1] * entering + x_ref[rows]
        high, low = split(entering)
        r = r_ref[:, cols]
        parts.append(base_ref[:, cols] + carry_ref[:, cols] * (dot(r, high) + dot(r, low)))
    gated = jnp.concatenate(parts, axis=1)
    gated_ref[...] = gated
    weight = rows_ref[1:2, :]
    stats_ref[...] = jnp.concatenate(to_lanes(gated * gated) + to_lanes(gated * weight), axis=0)


def keys_of(ref, k):
    return jnp.concatenate([ref[n, k + i, 0:64] for i in range(2) for n in range(4)], axis=0)


def values_of(ref, k):
    return jnp.concatenate([ref[n, k + i, 64:128] for i in range(2) for n in range(4)], axis=0)


def spread(q_ref, scaled_ref):
    c = math.log2(math.e) / math.sqrt(DIM)
    for h in range(2):
        high, low = split(q_ref[:, h * DIM : (h + 1) * DIM].astype(F32) * c)
        scaled_ref[pl.ds(h * 256, 256)] = jnp.concatenate([high, low], axis=1)


def scan_keys(kv_ref, core, scaled_ref, scores_ref, m_ref, l_ref, acc_ref, fresh):
    zl, here = lax.axis_index("zl"), lax.axis_index("core")
    tiles = zl + 1 if fresh else zl + here
    pairs = zl // 2 if fresh else tiles // 2
    rows = scaled_ref.shape[0]

    def lanes_max(s):
        return jnp.maximum(
            jnp.maximum(s[:, 0:128], s[:, 128:256]), jnp.maximum(s[:, 256:384], s[:, 384:512])
        )

    def scores(i):
        keys = keys_of(kv_ref, 2 * i)
        return dot(scaled_ref[...], jnp.concatenate([keys, keys], axis=1), 1, 1)

    def first(i, _):
        s = scores(i)
        scores_ref[i] = s
        m_ref[...] = jnp.maximum(m_ref[...], lanes_max(s))
        return 0

    def tail(i):
        key = lax.broadcasted_iota(jnp.int32, (rows, 512), 1)
        key = (i * 2) * 512 + core * 256 + jnp.where(key < 256, key, key + 256)
        spot = lax.broadcasted_iota(jnp.int32, (rows, 512), 0)
        spot = zl * 512 + here * 256 + jnp.where(spot < 256, spot, spot - 256)
        s = jnp.where(key <= spot, scores(i), NEG)
        scores_ref[i] = s
        m_ref[...] = jnp.maximum(m_ref[...], lanes_max(s))

    old = m_ref[...]
    lax.fori_loop(0, pairs, first, 0)
    ragged = 2 * pairs < tiles

    @pl.when(ragged)
    def _():
        tail(pairs)

    top = jnp.broadcast_to(jnp.max(m_ref[...], axis=1, keepdims=True), m_ref.shape)
    if fresh:
        l_ref[...] = jnp.zeros(l_ref.shape, F32)
        acc_ref[...] = jnp.zeros(acc_ref.shape, F32)
    else:
        fade = jnp.exp2(old - top)
        l_ref[...] = l_ref[...] * fade
        acc_ref[...] = acc_ref[...] * fade
    m_ref[...] = top

    def second(i, _):
        top = m_ref[...]
        p = [jnp.exp2(scores_ref[i, :, n : n + 128] - top) for n in range(0, 512, 128)]
        l_ref[...] += (p[0] + p[1]) + (p[2] + p[3])
        weights = jnp.concatenate([v.astype(BF16) for v in p], axis=1)
        acc_ref[...] += dot(weights, values_of(kv_ref, 2 * i))
        return 0

    lax.fori_loop(0, pairs + ragged.astype(jnp.int32), second, 0)


def attend_own_kernel(q_ref, kv_ref, scaled_ref, m_ref, l_ref, acc_ref, scores_ref):
    spread(q_ref, scaled_ref)
    m_ref[...] = jnp.full(m_ref.shape, NEG, F32)
    scan_keys(kv_ref, lax.axis_index("core"), scaled_ref, scores_ref, m_ref, l_ref, acc_ref, True)


def attend_other_kernel(
    scaled_ref, kv_ref, m_in, l_in, acc_in, rows_ref, stats_ref,
    o_ref, send_ref, m_ref, l_ref, acc_ref, scores_ref,
):
    m_ref[...] = m_in[...]
    l_ref[...] = l_in[...]
    acc_ref[...] = acc_in[...]
    other = 1 - lax.axis_index("core")
    scan_keys(kv_ref, other, scaled_ref, scores_ref, m_ref, l_ref, acc_ref, False)
    parts = []
    for h in range(2):
        at = pl.ds(h * 256, 256)
        parts.append(acc_ref[at] / jnp.sum(l_ref[at], axis=1, keepdims=True))
    attended = jnp.concatenate(parts, axis=1).astype(BF16)
    o_ref[...] = attended
    a = to_lanes(attended.astype(F32) * rows_ref[2:3, :])
    stats = jnp.concatenate([stats_ref[...]] + a + [jnp.zeros((2, DIM), F32)], axis=0)
    for n in range(send_ref.shape[0]):
        send_ref[n] = stats


def segment_row(values):
    full = jnp.concatenate([values, jnp.zeros((DIM - SEGMENTS, DIM), F32)], axis=0)
    return jnp.sum(jnp.transpose(full), axis=0, keepdims=True)


def middle_sums_kernel(got_ref, rows_ref, send_ref):
    total = got_ref[0]
    for n in range(1, got_ref.shape[0]):
        total = total + got_ref[n]
    segment = lax.broadcasted_iota(jnp.int32, (SEGMENTS, DIM), 0)
    seg = jnp.concatenate([rows_ref[3:4, :DIM], rows_ref[3:4, DIM:]], axis=0)
    held = seg.astype(jnp.int32)
    part = jnp.zeros((SEGMENTS, DIM), F32)
    for j in range(2):
        part = part + jnp.where(held[j : j + 1] == segment, total[4 + j : 5 + j], 0.0)
    part = segment_row(part)
    high = part.astype(BF16).astype(F32)
    out = jnp.concatenate([total[0:4], high, part - high, seg], axis=0).astype(BF16)
    for n in range(send_ref.shape[0]):
        send_ref[n] = out


def final_kernel(got_ref, gated_ref, rows_ref, o_ref, values_ref):
    index = lax.axis_index("zl") * 2 + lax.axis_index("core")
    mine = got_ref[2 * index].astype(F32) + got_ref[2 * index + 1].astype(F32)
    gain = rows_ref[0:1, :]
    for b in range(2):
        rows = pl.ds(b * DIM, DIM)
        scale = lax.rsqrt(mine[b : b + 1] * (1.0 / COLUMNS) + EPS)
        _, down = square(scale)
        for h in range(2):
            cols = slice(h * DIM, (h + 1) * DIM)
            o_ref[rows, cols] = (gated_ref[rows, cols] * down * gain[:, cols]).astype(BF16)
    segment = lax.broadcasted_iota(jnp.int32, (SEGMENTS, DIM), 0)
    part = jnp.zeros((SEGMENTS, DIM), F32)
    count = jnp.zeros((SEGMENTS, DIM), F32)
    extra = jnp.zeros((8, DIM), F32)
    for s in range(got_ref.shape[0] // 2):
        low = got_ref[2 * s].astype(F32)
        both = low + got_ref[2 * s + 1].astype(F32)
        extra = extra + both
        scale = lax.rsqrt(both[0:2] * (1.0 / COLUMNS) + EPS)
        score = scale * both[2:4]
        seg = low[6:8].astype(jnp.int32)
        for j in range(2):
            member = seg[j : j + 1] == segment
            part = part + jnp.where(member, score[j : j + 1], 0.0)
            count = count + jnp.where(member, 1.0, 0.0)
    total = segment_row(part) + extra[4:5] + extra[5:6]
    held = segment_row(count)
    values_ref[...] = (total / jnp.maximum(held, 1.0))[:, :SEGMENTS]


def per_device(
    queries,
    key_rows,
    value_rows,
    state_input,
    state_write,
    state_read,
    gate_input,
    decay_codes,
    decay_rates,
    skip_gain,
    norm_gain,
    attend_readout,
    state_readout,
    segment_index,
):
    tokens = queries.shape[0]
    codes = decay_codes.T
    seg = segment_index.reshape(1, 256)
    gain = norm_gain.reshape(1, 256)
    state_out = state_readout.reshape(1, 256)
    attend_out = attend_readout.reshape(1, 256)
    chips, wide = lax.axis_size("zl"), lax.axis_size("x")
    ctx = chips * lax.axis_size("core")

    together = lax.optimization_barrier
    packed = call(
        pack_kernel,
        shape((chips, DIM, DIM), BF16),
        [HBM] * 2,
        [pltpu.VMEM((DIM, DIM), BF16), pltpu.SemaphoreType.DMA((2,))],
        mib=PACK_MIB,
    )(key_rows, value_rows)
    packed, codes = together((packed, codes))
    quarter = lax.all_to_all(packed, "zl", 0, 0)
    own, send, rows = call(
        states_kernel,
        (shape((FADE + 8, DIM)), shape((STATE_ROWS, DIM), BF16), shape((8, 256))),
        [SMEM] + [VMEM] * 7,
    )(decay_rates, state_input, state_write, codes, gain, state_out, attend_out, seg)

    def shifted(v, by):
        return lax.ppermute(v, CTX, [(i, i + by) for i in range(ctx - by)])

    got = tuple(shifted(send, by) for by in (3, 2, 1))
    base, carry = call(
        local_kernel, (shape((tokens, 256)), shape((tokens, 256))), [VMEM] * 5 + [SMEM] * 2
    )(state_input, state_write, state_read, gate_input, codes, decay_rates, skip_gain)
    quarter, base = together((quarter, base))
    fan = call(fan_kernel, shape((wide, chips, DIM, DIM), BF16), [VMEM])(quarter)
    got, _ = together((got, fan))
    before, send = call(
        merge_kernel, (shape((FADE + 8, DIM)), shape((STATE_ROWS, DIM), BF16)), [VMEM] * 4, flops=MERGE_FLOPS
    )(*got[::-1], own)

    mine = lax.all_to_all(fan, "x", 0, 0)
    arrived = tuple(shifted(send, by) for by in (4, 8, 12))
    theirs = lax.ppermute(mine, "core", [(0, 1), (1, 0)])
    running = (shape((512, 256), BF16),) + (shape((512, DIM)),) * 3
    scores = pltpu.VMEM((chips // 2, 512, 512), F32)
    attention = call(attend_own_kernel, running, [VMEM] * 2, [scores], flops=10**9)(queries, mine)
    arrived, attention = together((arrived, attention))
    near, mid, far = arrived
    gated, stats = call(
        carried_kernel, (shape((tokens, 256)), shape((4, DIM))), [VMEM] * 8, flops=CARRIED_FLOPS
    )(near, mid, far, before, state_read, base, carry, rows)
    theirs, attention, stats = together((theirs, attention, stats))
    head_plane = lax.axis_size("y") * wide
    attended, send = call(
        attend_other_kernel,
        (shape((tokens, 256), BF16), shape((head_plane, 8, DIM))),
        [VMEM] * 7,
        [pltpu.VMEM((512, DIM), F32) for _ in range(3)] + [scores],
        flops=10**9,
    )(attention[0], theirs, *attention[1:], rows, stats)
    summed = lax.all_to_all(send, ("y", "x"), 0, 0)
    line = ctx * lax.axis_size("zh")
    send = call(middle_sums_kernel, shape((line, 8, DIM), BF16), [VMEM] * 2)(summed, rows)
    summed = lax.all_to_all(send, ("zl", "core", "zh"), 0, 0)
    state_mixed, values = call(
        final_kernel, (shape((tokens, 256), BF16), shape((1, SEGMENTS))), [VMEM] * 3
    )(summed, gated, rows)
    return attended, state_mixed, values.reshape(SEGMENTS)


def solution(mesh):
    grid = mesh.devices.shape
    inner = Mesh(mesh.devices.reshape(grid[0] // 2, 2, 2, 4, grid[1] // 8), CTX + HEAD)
    both = P(CTX, HEAD)
    rows, heads = P(CTX), P(HEAD)
    in_specs = (both, P(CTX, None), P(CTX, None)) + (both,) * 5 + (heads,) * 5 + (rows,)
    return jax.shard_map(
        per_device, mesh=inner, in_specs=in_specs, out_specs=(both, both, P()), check_vma=False
    )
```

```python
import functools
import math

import jax
import jax.numpy as jnp
from jax import lax
from jax.experimental import pallas as pl
from jax.experimental.pallas import tpu as pltpu
from jax.sharding import Mesh
from jax.sharding import PartitionSpec as P

HEADS = 64
KV_HEADS = 8
DIM = 128
BLOCK = 128
SEGMENTS = 32
COLUMNS = 8192
EPS = 1e-5

F32 = jnp.float32
BF16 = jnp.bfloat16
CTX = ("zl", "core")
HEAD = ("zh", "y", "x")
VMEM = pl.BlockSpec(memory_space=pltpu.VMEM)
SMEM = pl.BlockSpec(memory_space=pltpu.SMEM)
HBM = pl.BlockSpec(memory_space=pltpu.HBM)
NEG = -1e30
CARRIED_FLOPS = 10_800_000_000
MERGE_FLOPS = 20_000_000_000
PACK_MIB = 58
FADE = 2 * DIM
STATE_ROWS = FADE + 16


def call(kernel, outs, ins, scratch=(), flops=10**6, moved=10**6, mib=24):
    many = isinstance(outs, (tuple, list))
    return pl.pallas_call(
        kernel,
        out_shape=outs,
        in_specs=ins,
        out_specs=[VMEM] * len(outs) if many else VMEM,
        scratch_shapes=scratch,
        cost_estimate=pl.CostEstimate(flops=flops, bytes_accessed=moved, transcendentals=0),
        compiler_params=pltpu.CompilerParams(vmem_limit_bytes=int(mib * 2**20)),
    )


def shape(dims, kind=F32):
    return jax.ShapeDtypeStruct(dims, kind)


def dot(a, b, ca=1, cb=0):
    return lax.dot_general(a, b, (((ca,), (cb,)), ((), ())), preferred_element_type=F32)


def split(v):
    high = v.astype(BF16)
    return high, (v - high.astype(F32)).astype(BF16)


def code_sums(codes_ref):
    rows = []
    for b in range(2):
        part = codes_ref[:, b * BLOCK : (b + 1) * BLOCK]
        rows += [part >> 6, part & 63]
    stacked = jnp.concatenate(rows, axis=0).astype(F32).astype(BF16)
    upto = lax.broadcasted_iota(jnp.int32, (BLOCK, BLOCK), 0) <= lax.broadcasted_iota(
        jnp.int32, (BLOCK, BLOCK), 1
    )
    total = dot(stacked, jnp.where(upto, 1.0, 0.0).astype(BF16))
    sums = {}
    for b in range(2):
        for h in range(2):
            sums[b, h] = 64.0 * total[4 * b + h : 4 * b + h + 1] + total[4 * b + 2 + h : 4 * b + 3 + h]
    return sums


def square(row):
    lanes = jnp.broadcast_to(row, (DIM, DIM))
    return lanes, jnp.transpose(lanes)


def pack_kernel(k_hbm, v_hbm, packed_ref, piece, sems):
    group = lax.axis_index("zh") * 4 + lax.axis_index("y")
    quarter = pl.ds(pl.multiple_of(lax.axis_index("x") * 64, 64), 64)
    columns = pl.ds(pl.multiple_of(group * DIM, DIM), DIM)
    copies = [
        pltpu.make_async_copy(ref.at[quarter, columns], piece.at[pl.ds(64 * n, 64)], sems.at[n])
        for n, ref in enumerate((k_hbm, v_hbm))
    ]
    for c in copies:
        c.start()
    for c in copies:
        c.wait()
    both = piece[...]
    for n in range(packed_ref.shape[0]):
        packed_ref[n] = both


def states_kernel(
    rates_ref, x_ref, w_ref, codes_ref, gain_ref, state_out_ref, attend_out_ref, seg_ref,
    own_ref, send_ref, rows_ref,
):
    sums = code_sums(codes_ref)
    row = lax.broadcasted_iota(jnp.int32, (8, DIM), 0)
    fades, marks = jnp.zeros((8, DIM), F32), jnp.zeros((8, DIM), F32)
    for h in range(2):
        cols = pl.ds(h * DIM, DIM)
        rate = rates_ref[h]
        state = None
        whole = None
        for b in range(2):
            rows = pl.ds(b * BLOCK, BLOCK)
            _, down = square(sums[b, h])
            last = down[BLOCK - 1 : BLOCK]
            tail = jnp.exp(rate * (down - last))
            written = (w_ref[rows, cols].astype(F32) * tail).astype(BF16)
            added = dot(written, x_ref[rows, cols], 0, 0)
            fade = jnp.exp(-rate * last)
            state = added if b == 0 else fade * state + added
            whole = last if b == 0 else whole + last
        own_ref[pl.ds(h * DIM, DIM)] = state
        send_ref[pl.ds(h * DIM, DIM)] = state.astype(BF16)
        fade = jnp.exp(-rate * whole)
        high = fade.astype(BF16).astype(F32)
        marks = jnp.where(row == h, fade, marks)
        fades = jnp.where(row == 2 * h, high, jnp.where(row == 2 * h + 1, fade - high, fades))
    own_ref[pl.ds(FADE, 8)] = marks
    send_ref[pl.ds(FADE, 16)] = jnp.concatenate([fades, jnp.zeros((8, DIM), F32)], axis=0).astype(BF16)
    gain = gain_ref[...]
    rows_ref[...] = jnp.concatenate(
        [gain, gain * state_out_ref[...], attend_out_ref[...], seg_ref[...].astype(F32), jnp.zeros((4, 256), F32)],
        axis=0,
    )


def fan_kernel(quarter_ref, fan_ref):
    for n in range(fan_ref.shape[0]):
        fan_ref[n] = quarter_ref[...]


def merge_kernel(got1_ref, got2_ref, got3_ref, own_ref, x_out, send_ref):
    refs = (got1_ref, got2_ref, got3_ref)
    sent = [ref[pl.ds(FADE, 16)].astype(F32) for ref in refs]
    row = lax.broadcasted_iota(jnp.int32, (8, DIM), 0)
    fades, marks = jnp.zeros((8, DIM), F32), jnp.zeros((8, DIM), F32)
    for h in range(2):
        rows = pl.ds(h * DIM, DIM)
        f1, f2, f3 = (v[2 * h : 2 * h + 1] + v[2 * h + 1 : 2 * h + 2] for v in sent)
        g1, g2, g3 = (ref[rows].astype(F32) for ref in refs)
        before = g1 + f1 * (g2 + f2 * g3)
        x_out[rows] = before
        own = own_ref[pl.ds(FADE, 8)][h : h + 1]
        send_ref[rows] = (own * before + own_ref[rows]).astype(BF16)
        past = f1 * f2 * f3
        marks = jnp.where(row == h, past, marks)
        fade = own * past
        high = fade.astype(BF16).astype(F32)
        fades = jnp.where(row == 2 * h, high, jnp.where(row == 2 * h + 1, fade - high, fades))
    x_out[pl.ds(FADE, 8)] = marks
    send_ref[pl.ds(FADE, 16)] = jnp.concatenate([fades, jnp.zeros((8, DIM), F32)], axis=0).astype(BF16)


def local_kernel(x_ref, w_ref, r_ref, g_ref, codes_ref, rates_ref, skip_ref, base_ref, carry_ref):
    sums = code_sums(codes_ref)
    lower = lax.broadcasted_iota(jnp.int32, (BLOCK, BLOCK), 0) >= lax.broadcasted_iota(
        jnp.int32, (BLOCK, BLOCK), 1
    )
    for h in range(2):
        cols = pl.ds(h * DIM, DIM)
        rate, skip = rates_ref[h], skip_ref[h]
        state, before = None, None
        for b in range(2):
            rows = pl.ds(b * BLOCK, BLOCK)
            across, down = square(sums[b, h])
            x, w, r = x_ref[rows, cols], w_ref[rows, cols], r_ref[rows, cols]
            decay = jnp.exp(jnp.minimum(rate * (across - down), 0.0))
            scores = dot(r, w, 1, 1)
            mix = jnp.where(lower, scores * decay, 0.0).astype(BF16)
            y = dot(mix, x) + skip * x.astype(F32)
            if b == 0:
                last = down[BLOCK - 1 : BLOCK]
                tail = jnp.exp(rate * (down - last))
                state = dot((w.astype(F32) * tail).astype(BF16), x, 0, 0)
                before = last
                carry = jnp.exp(-rate * down)
            else:
                high, low = split(state)
                y = y + jnp.exp(-rate * down) * (dot(r, high) + dot(r, low))
                carry = jnp.exp(-rate * (down + before))
            gate = g_ref[rows, cols].astype(F32)
            silu = gate / (1.0 + jnp.exp(-gate))
            base_ref[rows, cols] = y * silu
            carry_ref[rows, cols] = carry * silu


def to_lanes(v):
    halves = v[:, :DIM] + v[:, DIM:]
    return [
        jnp.sum(jnp.transpose(halves[b * DIM : (b + 1) * DIM]), axis=0, keepdims=True)
        for b in range(2)
    ]


def carried_kernel(
    near_ref, mid_ref, far_ref, x_ref, r_ref, base_ref, carry_ref, rows_ref, gated_ref, stats_ref
):
    parts = []
    near, mid = near_ref[pl.ds(FADE, 16)].astype(F32), mid_ref[pl.ds(FADE, 16)].astype(F32)
    for h in range(2):
        rows, cols = pl.ds(h * DIM, DIM), pl.ds(h * DIM, DIM)
        entering = far_ref[rows].astype(F32)
        for ref, fades in ((mid_ref, mid), (near_ref, near)):
            fade = fades[2 * h : 2 * h + 1] + fades[2 * h + 1 : 2 * h + 2]
            entering = fade * entering + ref[rows].astype(F32)
        entering = x_ref[pl.ds(FADE, 8)][h : h + 1] * entering + x_ref[rows]
        high, low = split(entering)
        r = r_ref[:, cols]
        parts.append(base_ref[:, cols] + carry_ref[:, cols] * (dot(r, high) + dot(r, low)))
    gated = jnp.concatenate(parts, axis=1)
    gated_ref[...] = gated
    weight = rows_ref[1:2, :]
    stats_ref[...] = jnp.concatenate(to_lanes(gated * gated) + to_lanes(gated * weight), axis=0)


def keys_of(ref, k):
    return jnp.concatenate([ref[n, k + i, 0:64] for i in range(2) for n in range(4)], axis=0)


def values_of(ref, k):
    return jnp.concatenate([ref[n, k + i, 64:128] for i in range(2) for n in range(4)], axis=0)


def spread(q_ref, scaled_ref):
    c = math.log2(math.e) / math.sqrt(DIM)
    for h in range(2):
        high, low = split(q_ref[:, h * DIM : (h + 1) * DIM].astype(F32) * c)
        scaled_ref[pl.ds(h * 256, 256)] = jnp.concatenate([high, low], axis=1)


def scan_keys(kv_ref, core, scaled_ref, scores_ref, m_ref, l_ref, acc_ref, fresh):
    zl, here = lax.axis_index("zl"), lax.axis_index("core")
    tiles = zl + 1 if fresh else zl + here
    pairs = zl // 2 if fresh else tiles // 2
    rows = scaled_ref.shape[0]

    def lanes_max(s):
        return jnp.maximum(
            jnp.maximum(s[:, 0:128], s[:, 128:256]), jnp.maximum(s[:, 256:384], s[:, 384:512])
        )

    def scores(i):
        keys = keys_of(kv_ref, 2 * i)
        return dot(scaled_ref[...], jnp.concatenate([keys, keys], axis=1), 1, 1)

    def first(i, _):
        s = scores(i)
        scores_ref[i] = s
        m_ref[...] = jnp.maximum(m_ref[...], lanes_max(s))
        return 0

    def tail(i):
        key = lax.broadcasted_iota(jnp.int32, (rows, 512), 1)
        key = (i * 2) * 512 + core * 256 + jnp.where(key < 256, key, key + 256)
        spot = lax.broadcasted_iota(jnp.int32, (rows, 512), 0)
        spot = zl * 512 + here * 256 + jnp.where(spot < 256, spot, spot - 256)
        s = jnp.where(key <= spot, scores(i), NEG)
        scores_ref[i] = s
        m_ref[...] = jnp.maximum(m_ref[...], lanes_max(s))

    old = m_ref[...]
    lax.fori_loop(0, pairs, first, 0)
    ragged = 2 * pairs < tiles

    @pl.when(ragged)
    def _():
        tail(pairs)

    top = jnp.broadcast_to(jnp.max(m_ref[...], axis=1, keepdims=True), m_ref.shape)
    if fresh:
        l_ref[...] = jnp.zeros(l_ref.shape, F32)
        acc_ref[...] = jnp.zeros(acc_ref.shape, F32)
    else:
        fade = jnp.exp2(old - top)
        l_ref[...] = l_ref[...] * fade
        acc_ref[...] = acc_ref[...] * fade
    m_ref[...] = top

    def second(i, _):
        top = m_ref[...]
        p = [jnp.exp2(scores_ref[i, :, n : n + 128] - top) for n in range(0, 512, 128)]
        l_ref[...] += (p[0] + p[1]) + (p[2] + p[3])
        weights = jnp.concatenate([v.astype(BF16) for v in p], axis=1)
        acc_ref[...] += dot(weights, values_of(kv_ref, 2 * i))
        return 0

    lax.fori_loop(0, pairs + ragged.astype(jnp.int32), second, 0)


def attend_own_kernel(q_ref, kv_ref, scaled_ref, m_ref, l_ref, acc_ref, scores_ref):
    spread(q_ref, scaled_ref)
    m_ref[...] = jnp.full(m_ref.shape, NEG, F32)
    scan_keys(kv_ref, lax.axis_index("core"), scaled_ref, scores_ref, m_ref, l_ref, acc_ref, True)


def attend_other_kernel(
    scaled_ref, kv_ref, m_in, l_in, acc_in, rows_ref, stats_ref,
    o_ref, send_ref, m_ref, l_ref, acc_ref, scores_ref,
):
    m_ref[...] = m_in[...]
    l_ref[...] = l_in[...]
    acc_ref[...] = acc_in[...]
    other = 1 - lax.axis_index("core")
    scan_keys(kv_ref, other, scaled_ref, scores_ref, m_ref, l_ref, acc_ref, False)
    parts = []
    for h in range(2):
        at = pl.ds(h * 256, 256)
        parts.append(acc_ref[at] / jnp.sum(l_ref[at], axis=1, keepdims=True))
    attended = jnp.concatenate(parts, axis=1).astype(BF16)
    o_ref[...] = attended
    a = to_lanes(attended.astype(F32) * rows_ref[2:3, :])
    seg = [rows_ref[3:4, :DIM], rows_ref[3:4, DIM:]]
    stats = jnp.concatenate([stats_ref[...]] + a + seg, axis=0).astype(BF16)
    for n in range(send_ref.shape[0]):
        send_ref[n] = stats


def segment_row(values):
    full = jnp.concatenate([values, jnp.zeros((DIM - SEGMENTS, DIM), F32)], axis=0)
    return jnp.sum(jnp.transpose(full), axis=0, keepdims=True)


def middle_sums_kernel(got_ref, send_ref):
    segment = lax.broadcasted_iota(jnp.int32, (SEGMENTS, DIM), 0)
    plane = got_ref.shape[0] // 2
    rows = []
    for core in range(2):
        low = got_ref[core * plane].astype(F32)
        total = low
        for n in range(1, plane):
            total = total + got_ref[core * plane + n].astype(F32)
        seg = low[6:8]
        held = seg.astype(jnp.int32)
        part = jnp.zeros((SEGMENTS, DIM), F32)
        for j in range(2):
            part = part + jnp.where(held[j : j + 1] == segment, total[4 + j : 5 + j], 0.0)
        part = segment_row(part)
        high = part.astype(BF16).astype(F32)
        rows += [total[0:4], high, part - high, seg]
    out = jnp.concatenate(rows, axis=0).astype(BF16)
    for n in range(send_ref.shape[0]):
        send_ref[n] = out


def final_kernel(got_ref, gated_ref, rows_ref, o_ref, values_ref):
    zl, core = lax.axis_index("zl"), lax.axis_index("core")
    mine = got_ref[2 * zl].astype(F32) + got_ref[2 * zl + 1].astype(F32)
    mine = jnp.where(core == 0, mine[0:8], mine[8:16])
    gain = rows_ref[0:1, :]
    for b in range(2):
        rows = pl.ds(b * DIM, DIM)
        scale = lax.rsqrt(mine[b : b + 1] * (1.0 / COLUMNS) + EPS)
        _, down = square(scale)
        for h in range(2):
            cols = slice(h * DIM, (h + 1) * DIM)
            o_ref[rows, cols] = (gated_ref[rows, cols] * down * gain[:, cols]).astype(BF16)
    segment = lax.broadcasted_iota(jnp.int32, (SEGMENTS, DIM), 0)
    part = jnp.zeros((SEGMENTS, DIM), F32)
    count = jnp.zeros((SEGMENTS, DIM), F32)
    extra = jnp.zeros((8, DIM), F32)
    for s in range(got_ref.shape[0] // 2):
        low = got_ref[2 * s].astype(F32)
        pair = low + got_ref[2 * s + 1].astype(F32)
        for c in range(2):
            both = pair[8 * c : 8 * c + 8]
            extra = extra + both
            scale = lax.rsqrt(both[0:2] * (1.0 / COLUMNS) + EPS)
            score = scale * both[2:4]
            seg = low[8 * c + 6 : 8 * c + 8].astype(jnp.int32)
            for j in range(2):
                member = seg[j : j + 1] == segment
                part = part + jnp.where(member, score[j : j + 1], 0.0)
                count = count + jnp.where(member, 1.0, 0.0)
    total = segment_row(part) + extra[4:5] + extra[5:6]
    held = segment_row(count)
    values_ref[...] = (total / jnp.maximum(held, 1.0))[:, :SEGMENTS]


def per_device(
    queries,
    key_rows,
    value_rows,
    state_input,
    state_write,
    state_read,
    gate_input,
    decay_codes,
    decay_rates,
    skip_gain,
    norm_gain,
    attend_readout,
    state_readout,
    segment_index,
):
    tokens = queries.shape[0]
    codes = decay_codes.T
    seg = segment_index.reshape(1, 256)
    gain = norm_gain.reshape(1, 256)
    state_out = state_readout.reshape(1, 256)
    attend_out = attend_readout.reshape(1, 256)
    chips, wide = lax.axis_size("zl"), lax.axis_size("x")
    ctx = chips * lax.axis_size("core")

    together = lax.optimization_barrier
    packed = call(
        pack_kernel,
        shape((chips, DIM, DIM), BF16),
        [HBM] * 2,
        [pltpu.VMEM((DIM, DIM), BF16), pltpu.SemaphoreType.DMA((2,))],
        mib=PACK_MIB,
    )(key_rows, value_rows)
    packed, codes = together((packed, codes))
    quarter = lax.all_to_all(packed, "zl", 0, 0)
    own, send, rows = call(
        states_kernel,
        (shape((FADE + 8, DIM)), shape((STATE_ROWS, DIM), BF16), shape((8, 256))),
        [SMEM] + [VMEM] * 7,
    )(decay_rates, state_input, state_write, codes, gain, state_out, attend_out, seg)

    def shifted(v, by):
        return lax.ppermute(v, CTX, [(i, i + by) for i in range(ctx - by)])

    got = tuple(shifted(send, by) for by in (3, 2, 1))
    base, carry = call(
        local_kernel, (shape((tokens, 256)), shape((tokens, 256))), [VMEM] * 5 + [SMEM] * 2
    )(state_input, state_write, state_read, gate_input, codes, decay_rates, skip_gain)
    quarter, base = together((quarter, base))
    fan = call(fan_kernel, shape((wide, chips, DIM, DIM), BF16), [VMEM])(quarter)
    got, _ = together((got, fan))
    before, send = call(
        merge_kernel, (shape((FADE + 8, DIM)), shape((STATE_ROWS, DIM), BF16)), [VMEM] * 4, flops=MERGE_FLOPS
    )(*got[::-1], own)

    mine = lax.all_to_all(fan, "x", 0, 0)
    arrived = tuple(shifted(send, by) for by in (4, 8, 12))
    theirs = lax.ppermute(mine, "core", [(0, 1), (1, 0)])
    running = (shape((512, 256), BF16),) + (shape((512, DIM)),) * 3
    scores = pltpu.VMEM((chips // 2, 512, 512), F32)
    attention = call(attend_own_kernel, running, [VMEM] * 2, [scores], flops=10**9)(queries, mine)
    arrived, attention = together((arrived, attention))
    near, mid, far = arrived
    gated, stats = call(
        carried_kernel, (shape((tokens, 256)), shape((4, DIM))), [VMEM] * 8, flops=CARRIED_FLOPS
    )(near, mid, far, before, state_read, base, carry, rows)
    theirs, attention, stats = together((theirs, attention, stats))
    head_plane = lax.axis_size("y") * wide
    attended, send = call(
        attend_other_kernel,
        (shape((tokens, 256), BF16), shape((2 * head_plane, 8, DIM), BF16)),
        [VMEM] * 7,
        [pltpu.VMEM((512, DIM), F32) for _ in range(3)] + [scores],
        flops=10**9,
    )(attention[0], theirs, *attention[1:], rows, stats)
    summed = lax.all_to_all(send, ("core", "y", "x"), 0, 0)
    line = chips * lax.axis_size("zh")
    send = call(middle_sums_kernel, shape((line, 16, DIM), BF16), [VMEM])(summed)
    summed = lax.all_to_all(send, ("zl", "zh"), 0, 0)
    state_mixed, values = call(
        final_kernel, (shape((tokens, 256), BF16), shape((1, SEGMENTS))), [VMEM] * 3
    )(summed, gated, rows)
    return attended, state_mixed, values.reshape(SEGMENTS)


def solution(mesh):
    grid = mesh.devices.shape
    inner = Mesh(mesh.devices.reshape(grid[0] // 2, 2, 2, 4, grid[1] // 8), CTX + HEAD)
    both = P(CTX, HEAD)
    rows, heads = P(CTX), P(HEAD)
    in_specs = (both, P(CTX, None), P(CTX, None)) + (both,) * 5 + (heads,) * 5 + (rows,)
    return jax.shard_map(
        per_device, mesh=inner, in_specs=in_specs, out_specs=(both, both, P()), check_vma=False
    )
```

```python
import functools
import math

import jax
import jax.numpy as jnp
from jax import lax
from jax.experimental import pallas as pl
from jax.experimental.pallas import tpu as pltpu
from jax.sharding import Mesh
from jax.sharding import PartitionSpec as P

HEADS = 64
KV_HEADS = 8
DIM = 128
BLOCK = 128
SEGMENTS = 32
COLUMNS = 8192
EPS = 1e-5

F32 = jnp.float32
BF16 = jnp.bfloat16
CTX = ("zl", "core")
HEAD = ("zh", "y", "x")
VMEM = pl.BlockSpec(memory_space=pltpu.VMEM)
SMEM = pl.BlockSpec(memory_space=pltpu.SMEM)
HBM = pl.BlockSpec(memory_space=pltpu.HBM)
NEG = -1e30
CARRIED_FLOPS = 10_800_000_000
MERGE_FLOPS = 20_000_000_000
PACK_MIB = 58
FADE = 2 * DIM
STATE_ROWS = FADE + 16


def call(kernel, outs, ins, scratch=(), flops=10**6, moved=10**6, mib=24):
    many = isinstance(outs, (tuple, list))
    return pl.pallas_call(
        kernel,
        out_shape=outs,
        in_specs=ins,
        out_specs=[VMEM] * len(outs) if many else VMEM,
        scratch_shapes=scratch,
        cost_estimate=pl.CostEstimate(flops=flops, bytes_accessed=moved, transcendentals=0),
        compiler_params=pltpu.CompilerParams(vmem_limit_bytes=int(mib * 2**20)),
    )


def shape(dims, kind=F32):
    return jax.ShapeDtypeStruct(dims, kind)


def dot(a, b, ca=1, cb=0):
    return lax.dot_general(a, b, (((ca,), (cb,)), ((), ())), preferred_element_type=F32)


def split(v):
    high = v.astype(BF16)
    return high, (v - high.astype(F32)).astype(BF16)


def code_sums(codes_ref):
    rows = []
    for b in range(2):
        part = codes_ref[:, b * BLOCK : (b + 1) * BLOCK]
        rows += [part >> 6, part & 63]
    stacked = jnp.concatenate(rows, axis=0).astype(F32).astype(BF16)
    upto = lax.broadcasted_iota(jnp.int32, (BLOCK, BLOCK), 0) <= lax.broadcasted_iota(
        jnp.int32, (BLOCK, BLOCK), 1
    )
    total = dot(stacked, jnp.where(upto, 1.0, 0.0).astype(BF16))
    sums = {}
    for b in range(2):
        for h in range(2):
            sums[b, h] = 64.0 * total[4 * b + h : 4 * b + h + 1] + total[4 * b + 2 + h : 4 * b + 3 + h]
    return sums


def square(row):
    lanes = jnp.broadcast_to(row, (DIM, DIM))
    return lanes, jnp.transpose(lanes)


def pack_kernel(k_hbm, v_hbm, packed_ref, piece, sems):
    group = lax.axis_index("zh") * 4 + lax.axis_index("y")
    quarter = pl.ds(pl.multiple_of(lax.axis_index("x") * 64, 64), 64)
    columns = pl.ds(pl.multiple_of(group * DIM, DIM), DIM)
    copies = [
        pltpu.make_async_copy(ref.at[quarter, columns], piece.at[pl.ds(64 * n, 64)], sems.at[n])
        for n, ref in enumerate((k_hbm, v_hbm))
    ]
    for c in copies:
        c.start()
    for c in copies:
        c.wait()
    both = piece[...]
    for n in range(packed_ref.shape[0]):
        packed_ref[n] = both


def states_kernel(
    rates_ref, x_ref, w_ref, codes_ref, gain_ref, state_out_ref, attend_out_ref, seg_ref,
    own_ref, send_ref, rows_ref,
):
    sums = code_sums(codes_ref)
    row = lax.broadcasted_iota(jnp.int32, (8, DIM), 0)
    fades, marks = jnp.zeros((8, DIM), F32), jnp.zeros((8, DIM), F32)
    for h in range(2):
        cols = pl.ds(h * DIM, DIM)
        rate = rates_ref[h]
        state = None
        whole = None
        for b in range(2):
            rows = pl.ds(b * BLOCK, BLOCK)
            _, down = square(sums[b, h])
            last = down[BLOCK - 1 : BLOCK]
            tail = jnp.exp(rate * (down - last))
            written = (w_ref[rows, cols].astype(F32) * tail).astype(BF16)
            added = dot(written, x_ref[rows, cols], 0, 0)
            fade = jnp.exp(-rate * last)
            state = added if b == 0 else fade * state + added
            whole = last if b == 0 else whole + last
        own_ref[pl.ds(h * DIM, DIM)] = state
        send_ref[pl.ds(h * DIM, DIM)] = state.astype(BF16)
        fade = jnp.exp(-rate * whole)
        high = fade.astype(BF16).astype(F32)
        marks = jnp.where(row == h, fade, marks)
        fades = jnp.where(row == 2 * h, high, jnp.where(row == 2 * h + 1, fade - high, fades))
    own_ref[pl.ds(FADE, 8)] = marks
    send_ref[pl.ds(FADE, 16)] = jnp.concatenate([fades, jnp.zeros((8, DIM), F32)], axis=0).astype(BF16)
    gain = gain_ref[...]
    rows_ref[...] = jnp.concatenate(
        [gain, gain * state_out_ref[...], attend_out_ref[...], seg_ref[...].astype(F32), jnp.zeros((4, 256), F32)],
        axis=0,
    )


def fan_kernel(quarter_ref, fan_ref):
    for n in range(fan_ref.shape[0]):
        fan_ref[n] = quarter_ref[...]


def merge_kernel(got1_ref, got2_ref, got3_ref, own_ref, x_out, send_ref):
    refs = (got1_ref, got2_ref, got3_ref)
    sent = [ref[pl.ds(FADE, 16)].astype(F32) for ref in refs]
    row = lax.broadcasted_iota(jnp.int32, (8, DIM), 0)
    fades, marks = jnp.zeros((8, DIM), F32), jnp.zeros((8, DIM), F32)
    for h in range(2):
        rows = pl.ds(h * DIM, DIM)
        f1, f2, f3 = (v[2 * h : 2 * h + 1] + v[2 * h + 1 : 2 * h + 2] for v in sent)
        g1, g2, g3 = (ref[rows].astype(F32) for ref in refs)
        before = g1 + f1 * (g2 + f2 * g3)
        x_out[rows] = before
        own = own_ref[pl.ds(FADE, 8)][h : h + 1]
        send_ref[rows] = (own * before + own_ref[rows]).astype(BF16)
        past = f1 * f2 * f3
        marks = jnp.where(row == h, past, marks)
        fade = own * past
        high = fade.astype(BF16).astype(F32)
        fades = jnp.where(row == 2 * h, high, jnp.where(row == 2 * h + 1, fade - high, fades))
    x_out[pl.ds(FADE, 8)] = marks
    send_ref[pl.ds(FADE, 16)] = jnp.concatenate([fades, jnp.zeros((8, DIM), F32)], axis=0).astype(BF16)


def local_kernel(x_ref, w_ref, r_ref, g_ref, codes_ref, rates_ref, skip_ref, base_ref, carry_ref):
    sums = code_sums(codes_ref)
    lower = lax.broadcasted_iota(jnp.int32, (BLOCK, BLOCK), 0) >= lax.broadcasted_iota(
        jnp.int32, (BLOCK, BLOCK), 1
    )
    for h in range(2):
        cols = pl.ds(h * DIM, DIM)
        rate, skip = rates_ref[h], skip_ref[h]
        state, before = None, None
        for b in range(2):
            rows = pl.ds(b * BLOCK, BLOCK)
            across, down = square(sums[b, h])
            x, w, r = x_ref[rows, cols], w_ref[rows, cols], r_ref[rows, cols]
            decay = jnp.exp(jnp.minimum(rate * (across - down), 0.0))
            scores = dot(r, w, 1, 1)
            mix = jnp.where(lower, scores * decay, 0.0).astype(BF16)
            y = dot(mix, x) + skip * x.astype(F32)
            if b == 0:
                last = down[BLOCK - 1 : BLOCK]
                tail = jnp.exp(rate * (down - last))
                state = dot((w.astype(F32) * tail).astype(BF16), x, 0, 0)
                before = last
                carry = jnp.exp(-rate * down)
            else:
                high, low = split(state)
                y = y + jnp.exp(-rate * down) * (dot(r, high) + dot(r, low))
                carry = jnp.exp(-rate * (down + before))
            gate = g_ref[rows, cols].astype(F32)
            silu = gate / (1.0 + jnp.exp(-gate))
            base_ref[rows, cols] = y * silu
            carry_ref[rows, cols] = carry * silu


def to_lanes(v):
    halves = v[:, :DIM] + v[:, DIM:]
    return [
        jnp.sum(jnp.transpose(halves[b * DIM : (b + 1) * DIM]), axis=0, keepdims=True)
        for b in range(2)
    ]


def carried_kernel(
    near_ref, mid_ref, far_ref, x_ref, r_ref, base_ref, carry_ref, rows_ref, gated_ref, stats_ref
):
    parts = []
    near, mid = near_ref[pl.ds(FADE, 16)].astype(F32), mid_ref[pl.ds(FADE, 16)].astype(F32)
    for h in range(2):
        rows, cols = pl.ds(h * DIM, DIM), pl.ds(h * DIM, DIM)
        entering = far_ref[rows].astype(F32)
        for ref, fades in ((mid_ref, mid), (near_ref, near)):
            fade = fades[2 * h : 2 * h + 1] + fades[2 * h + 1 : 2 * h + 2]
            entering = fade * entering + ref[rows].astype(F32)
        entering = x_ref[pl.ds(FADE, 8)][h : h + 1] * entering + x_ref[rows]
        high, low = split(entering)
        r = r_ref[:, cols]
        parts.append(base_ref[:, cols] + carry_ref[:, cols] * (dot(r, high) + dot(r, low)))
    gated = jnp.concatenate(parts, axis=1)
    gated_ref[...] = gated
    weight = rows_ref[1:2, :]
    stats_ref[...] = jnp.concatenate(to_lanes(gated * gated) + to_lanes(gated * weight), axis=0)


def keys_of(ref, k):
    return jnp.concatenate([ref[n, k + i, 0:64] for i in range(2) for n in range(4)], axis=0)


def values_of(ref, k):
    return jnp.concatenate([ref[n, k + i, 64:128] for i in range(2) for n in range(4)], axis=0)


def spread(q_ref, scaled_ref):
    c = math.log2(math.e) / math.sqrt(DIM)
    for h in range(2):
        high, low = split(q_ref[:, h * DIM : (h + 1) * DIM].astype(F32) * c)
        scaled_ref[pl.ds(h * 256, 256)] = jnp.concatenate([high, low], axis=1)


def scan_keys(kv_ref, core, scaled_ref, scores_ref, m_ref, l_ref, acc_ref, fresh):
    zl, here = lax.axis_index("zl"), lax.axis_index("core")
    tiles = zl + 1 if fresh else zl + here
    pairs = zl // 2 if fresh else tiles // 2
    rows = scaled_ref.shape[0]

    def lanes_max(s):
        return jnp.maximum(
            jnp.maximum(s[:, 0:128], s[:, 128:256]), jnp.maximum(s[:, 256:384], s[:, 384:512])
        )

    def scores(i):
        keys = keys_of(kv_ref, 2 * i)
        return dot(scaled_ref[...], jnp.concatenate([keys, keys], axis=1), 1, 1)

    def first(i, _):
        s = scores(i)
        scores_ref[i] = s
        m_ref[...] = jnp.maximum(m_ref[...], lanes_max(s))
        return 0

    def tail(i):
        key = lax.broadcasted_iota(jnp.int32, (rows, 512), 1)
        key = (i * 2) * 512 + core * 256 + jnp.where(key < 256, key, key + 256)
        spot = lax.broadcasted_iota(jnp.int32, (rows, 512), 0)
        spot = zl * 512 + here * 256 + jnp.where(spot < 256, spot, spot - 256)
        s = jnp.where(key <= spot, scores(i), NEG)
        scores_ref[i] = s
        m_ref[...] = jnp.maximum(m_ref[...], lanes_max(s))

    old = m_ref[...]
    lax.fori_loop(0, pairs, first, 0)
    ragged = 2 * pairs < tiles

    @pl.when(ragged)
    def _():
        tail(pairs)

    top = jnp.broadcast_to(jnp.max(m_ref[...], axis=1, keepdims=True), m_ref.shape)
    if fresh:
        l_ref[...] = jnp.zeros(l_ref.shape, F32)
        acc_ref[...] = jnp.zeros(acc_ref.shape, F32)
    else:
        fade = jnp.exp2(old - top)
        l_ref[...] = l_ref[...] * fade
        acc_ref[...] = acc_ref[...] * fade
    m_ref[...] = top

    def second(i, _):
        top = m_ref[...]
        p = [jnp.exp2(scores_ref[i, :, n : n + 128] - top) for n in range(0, 512, 128)]
        l_ref[...] += (p[0] + p[1]) + (p[2] + p[3])
        weights = jnp.concatenate([v.astype(BF16) for v in p], axis=1)
        acc_ref[...] += dot(weights, values_of(kv_ref, 2 * i))
        return 0

    lax.fori_loop(0, pairs + ragged.astype(jnp.int32), second, 0)


def attend_own_kernel(q_ref, kv_ref, scaled_ref, m_ref, l_ref, acc_ref, scores_ref):
    spread(q_ref, scaled_ref)
    m_ref[...] = jnp.full(m_ref.shape, NEG, F32)
    scan_keys(kv_ref, lax.axis_index("core"), scaled_ref, scores_ref, m_ref, l_ref, acc_ref, True)


def attend_other_kernel(
    scaled_ref, kv_ref, m_in, l_in, acc_in, rows_ref, stats_ref,
    o_ref, send_ref, m_ref, l_ref, acc_ref, scores_ref,
):
    m_ref[...] = m_in[...]
    l_ref[...] = l_in[...]
    acc_ref[...] = acc_in[...]
    other = 1 - lax.axis_index("core")
    scan_keys(kv_ref, other, scaled_ref, scores_ref, m_ref, l_ref, acc_ref, False)
    parts = []
    for h in range(2):
        at = pl.ds(h * 256, 256)
        parts.append(acc_ref[at] / jnp.sum(l_ref[at], axis=1, keepdims=True))
    attended = jnp.concatenate(parts, axis=1).astype(BF16)
    o_ref[...] = attended
    a = to_lanes(attended.astype(F32) * rows_ref[2:3, :])
    seg = [rows_ref[3:4, :DIM], rows_ref[3:4, DIM:]]
    stats = jnp.concatenate([stats_ref[...]] + a + seg, axis=0).astype(BF16)
    for n in range(send_ref.shape[0]):
        send_ref[n] = stats


def segment_row(values):
    full = jnp.concatenate([values, jnp.zeros((DIM - SEGMENTS, DIM), F32)], axis=0)
    return jnp.sum(jnp.transpose(full), axis=0, keepdims=True)


def middle_sums_kernel(got_ref, send_ref):
    segment = lax.broadcasted_iota(jnp.int32, (SEGMENTS, DIM), 0)
    plane = got_ref.shape[0] // 2
    rows = []
    for core in range(2):
        low = got_ref[core * plane].astype(F32)
        total = low
        for n in range(1, plane):
            total = total + got_ref[core * plane + n].astype(F32)
        seg = low[6:8]
        held = seg.astype(jnp.int32)
        part = jnp.zeros((SEGMENTS, DIM), F32)
        for j in range(2):
            part = part + jnp.where(held[j : j + 1] == segment, total[4 + j : 5 + j], 0.0)
        part = segment_row(part)
        high = part.astype(BF16).astype(F32)
        rows += [total[0:4], high, part - high, seg]
    out = jnp.concatenate(rows, axis=0).astype(BF16)
    for n in range(send_ref.shape[0]):
        send_ref[n] = out


def final_kernel(got_ref, gated_ref, rows_ref, o_ref, values_ref):
    zl, core = lax.axis_index("zl"), lax.axis_index("core")
    mine = got_ref[2 * zl].astype(F32) + got_ref[2 * zl + 1].astype(F32)
    mine = jnp.where(core == 0, mine[0:8], mine[8:16])
    gain = rows_ref[0:1, :]
    for b in range(2):
        rows = pl.ds(b * DIM, DIM)
        scale = lax.rsqrt(mine[b : b + 1] * (1.0 / COLUMNS) + EPS)
        _, down = square(scale)
        for h in range(2):
            cols = slice(h * DIM, (h + 1) * DIM)
            o_ref[rows, cols] = (gated_ref[rows, cols] * down * gain[:, cols]).astype(BF16)
    segment = lax.broadcasted_iota(jnp.int32, (SEGMENTS, DIM), 0)
    part = jnp.zeros((SEGMENTS, DIM), F32)
    count = jnp.zeros((SEGMENTS, DIM), F32)
    extra = jnp.zeros((8, DIM), F32)
    for s in range(got_ref.shape[0] // 2):
        low = got_ref[2 * s].astype(F32)
        pair = low + got_ref[2 * s + 1].astype(F32)
        for c in range(2):
            both = pair[8 * c : 8 * c + 8]
            extra = extra + both
            scale = lax.rsqrt(both[0:2] * (1.0 / COLUMNS) + EPS)
            score = scale * both[2:4]
            seg = low[8 * c + 6 : 8 * c + 8].astype(jnp.int32)
            for j in range(2):
                member = seg[j : j + 1] == segment
                part = part + jnp.where(member, score[j : j + 1], 0.0)
                count = count + jnp.where(member, 1.0, 0.0)
    total = segment_row(part) + extra[4:5] + extra[5:6]
    held = segment_row(count)
    values_ref[...] = (total / jnp.maximum(held, 1.0))[:, :SEGMENTS]


def per_device(
    queries,
    key_rows,
    value_rows,
    state_input,
    state_write,
    state_read,
    gate_input,
    decay_codes,
    decay_rates,
    skip_gain,
    norm_gain,
    attend_readout,
    state_readout,
    segment_index,
):
    tokens = queries.shape[0]
    codes = decay_codes.T
    seg = segment_index.reshape(1, 256)
    gain = norm_gain.reshape(1, 256)
    state_out = state_readout.reshape(1, 256)
    attend_out = attend_readout.reshape(1, 256)
    chips, wide = lax.axis_size("zl"), lax.axis_size("x")
    ctx = chips * lax.axis_size("core")

    together = lax.optimization_barrier
    packed = call(
        pack_kernel,
        shape((chips, DIM, DIM), BF16),
        [HBM] * 2,
        [pltpu.VMEM((DIM, DIM), BF16), pltpu.SemaphoreType.DMA((2,))],
        mib=PACK_MIB,
    )(key_rows, value_rows)
    packed, codes = together((packed, codes))
    quarter = lax.all_to_all(packed, "zl", 0, 0)
    own, send, rows = call(
        states_kernel,
        (shape((FADE + 8, DIM)), shape((STATE_ROWS, DIM), BF16), shape((8, 256))),
        [SMEM] + [VMEM] * 7,
    )(decay_rates, state_input, state_write, codes, gain, state_out, attend_out, seg)

    def shifted(v, by):
        return lax.ppermute(v, CTX, [(i, i + by) for i in range(ctx - by)])

    got = tuple(shifted(send, by) for by in (3, 2, 1))
    base, carry = call(
        local_kernel, (shape((tokens, 256)), shape((tokens, 256))), [VMEM] * 5 + [SMEM] * 2
    )(state_input, state_write, state_read, gate_input, codes, decay_rates, skip_gain)
    quarter, base = together((quarter, base))
    fan = call(fan_kernel, shape((wide, chips, DIM, DIM), BF16), [VMEM])(quarter)
    got, _ = together((got, fan))
    before, send = call(
        merge_kernel, (shape((FADE + 8, DIM)), shape((STATE_ROWS, DIM), BF16)), [VMEM] * 4, flops=MERGE_FLOPS
    )(*got[::-1], own)

    mine = lax.all_to_all(fan, "x", 0, 0)
    arrived = tuple(shifted(send, by) for by in (4, 12, 8))
    theirs = lax.ppermute(mine, "core", [(0, 1), (1, 0)])
    running = (shape((512, 256), BF16),) + (shape((512, DIM)),) * 3
    scores = pltpu.VMEM((chips // 2, 512, 512), F32)
    attention = call(attend_own_kernel, running, [VMEM] * 2, [scores], flops=10**9)(queries, mine)
    arrived, attention = together((arrived, attention))
    near, far, mid = arrived
    gated, stats = call(
        carried_kernel, (shape((tokens, 256)), shape((4, DIM))), [VMEM] * 8, flops=CARRIED_FLOPS
    )(near, mid, far, before, state_read, base, carry, rows)
    theirs, attention, stats = together((theirs, attention, stats))
    head_plane = lax.axis_size("y") * wide
    attended, send = call(
        attend_other_kernel,
        (shape((tokens, 256), BF16), shape((2 * head_plane, 8, DIM), BF16)),
        [VMEM] * 7,
        [pltpu.VMEM((512, DIM), F32) for _ in range(3)] + [scores],
        flops=10**9,
    )(attention[0], theirs, *attention[1:], rows, stats)
    summed = lax.all_to_all(send, ("core", "y", "x"), 0, 0)
    line = chips * lax.axis_size("zh")
    send = call(middle_sums_kernel, shape((line, 16, DIM), BF16), [VMEM])(summed)
    summed = lax.all_to_all(send, ("zl", "zh"), 0, 0)
    state_mixed, values = call(
        final_kernel, (shape((tokens, 256), BF16), shape((1, SEGMENTS))), [VMEM] * 3
    )(summed, gated, rows)
    return attended, state_mixed, values.reshape(SEGMENTS)


def solution(mesh):
    grid = mesh.devices.shape
    inner = Mesh(mesh.devices.reshape(grid[0] // 2, 2, 2, 4, grid[1] // 8), CTX + HEAD)
    both = P(CTX, HEAD)
    rows, heads = P(CTX), P(HEAD)
    in_specs = (both, P(CTX, None), P(CTX, None)) + (both,) * 5 + (heads,) * 5 + (rows,)
    return jax.shard_map(
        per_device, mesh=inner, in_specs=in_specs, out_specs=(both, both, P()), check_vma=False
    )
```

```python
import functools
import math

import jax
import jax.numpy as jnp
from jax import lax
from jax.experimental import pallas as pl
from jax.experimental.pallas import tpu as pltpu
from jax.sharding import Mesh
from jax.sharding import PartitionSpec as P

HEADS = 64
KV_HEADS = 8
DIM = 128
BLOCK = 128
SEGMENTS = 32
COLUMNS = 8192
EPS = 1e-5

F32 = jnp.float32
BF16 = jnp.bfloat16
CTX = ("zl", "core")
HEAD = ("zh", "y", "x")
VMEM = pl.BlockSpec(memory_space=pltpu.VMEM)
SMEM = pl.BlockSpec(memory_space=pltpu.SMEM)
HBM = pl.BlockSpec(memory_space=pltpu.HBM)
NEG = -1e30
CARRIED_FLOPS = 10_800_000_000
MERGE_FLOPS = 20_000_000_000
PACK_MIB = 58
FADE = 2 * DIM
STATE_ROWS = FADE + 16


def call(kernel, outs, ins, scratch=(), flops=10**6, moved=10**6, mib=24):
    many = isinstance(outs, (tuple, list))
    return pl.pallas_call(
        kernel,
        out_shape=outs,
        in_specs=ins,
        out_specs=[VMEM] * len(outs) if many else VMEM,
        scratch_shapes=scratch,
        cost_estimate=pl.CostEstimate(flops=flops, bytes_accessed=moved, transcendentals=0),
        compiler_params=pltpu.CompilerParams(vmem_limit_bytes=int(mib * 2**20)),
    )


def shape(dims, kind=F32):
    return jax.ShapeDtypeStruct(dims, kind)


def dot(a, b, ca=1, cb=0):
    return lax.dot_general(a, b, (((ca,), (cb,)), ((), ())), preferred_element_type=F32)


def split(v):
    high = v.astype(BF16)
    return high, (v - high.astype(F32)).astype(BF16)


def code_sums(codes_ref):
    rows = []
    for b in range(2):
        part = codes_ref[:, b * BLOCK : (b + 1) * BLOCK]
        rows += [part >> 6, part & 63]
    stacked = jnp.concatenate(rows, axis=0).astype(F32).astype(BF16)
    upto = lax.broadcasted_iota(jnp.int32, (BLOCK, BLOCK), 0) <= lax.broadcasted_iota(
        jnp.int32, (BLOCK, BLOCK), 1
    )
    total = dot(stacked, jnp.where(upto, 1.0, 0.0).astype(BF16))
    sums = {}
    for b in range(2):
        for h in range(2):
            sums[b, h] = 64.0 * total[4 * b + h : 4 * b + h + 1] + total[4 * b + 2 + h : 4 * b + 3 + h]
    return sums


def square(row):
    lanes = jnp.broadcast_to(row, (DIM, DIM))
    return lanes, jnp.transpose(lanes)


def pack_kernel(k_hbm, v_hbm, packed_ref, piece, sems):
    group = lax.axis_index("zh") * 4 + lax.axis_index("y")
    quarter = pl.ds(pl.multiple_of(lax.axis_index("x") * 64, 64), 64)
    columns = pl.ds(pl.multiple_of(group * DIM, DIM), DIM)
    copies = [
        pltpu.make_async_copy(ref.at[quarter, columns], piece.at[pl.ds(64 * n, 64)], sems.at[n])
        for n, ref in enumerate((k_hbm, v_hbm))
    ]
    for c in copies:
        c.start()
    for c in copies:
        c.wait()
    both = piece[...]
    for n in range(packed_ref.shape[0]):
        packed_ref[n] = both


def states_kernel(
    rates_ref, x_ref, w_ref, codes_ref, gain_ref, state_out_ref, attend_out_ref, seg_ref,
    own_ref, send_ref, rows_ref,
):
    sums = code_sums(codes_ref)
    row = lax.broadcasted_iota(jnp.int32, (8, DIM), 0)
    fades, marks = jnp.zeros((8, DIM), F32), jnp.zeros((8, DIM), F32)
    for h in range(2):
        cols = pl.ds(h * DIM, DIM)
        rate = rates_ref[h]
        state = None
        whole = None
        for b in range(2):
            rows = pl.ds(b * BLOCK, BLOCK)
            _, down = square(sums[b, h])
            last = down[BLOCK - 1 : BLOCK]
            tail = jnp.exp(rate * (down - last))
            written = (w_ref[rows, cols].astype(F32) * tail).astype(BF16)
            added = dot(written, x_ref[rows, cols], 0, 0)
            fade = jnp.exp(-rate * last)
            state = added if b == 0 else fade * state + added
            whole = last if b == 0 else whole + last
        own_ref[pl.ds(h * DIM, DIM)] = state
        send_ref[pl.ds(h * DIM, DIM)] = state.astype(BF16)
        fade = jnp.exp(-rate * whole)
        high = fade.astype(BF16).astype(F32)
        marks = jnp.where(row == h, fade, marks)
        fades = jnp.where(row == 2 * h, high, jnp.where(row == 2 * h + 1, fade - high, fades))
    own_ref[pl.ds(FADE, 8)] = marks
    send_ref[pl.ds(FADE, 16)] = jnp.concatenate([fades, jnp.zeros((8, DIM), F32)], axis=0).astype(BF16)
    gain = gain_ref[...]
    rows_ref[...] = jnp.concatenate(
        [gain, gain * state_out_ref[...], attend_out_ref[...], seg_ref[...].astype(F32), jnp.zeros((4, 256), F32)],
        axis=0,
    )


def fan_kernel(quarter_ref, fan_ref):
    for n in range(fan_ref.shape[0]):
        fan_ref[n] = quarter_ref[...]


def merge_kernel(got1_ref, got2_ref, got3_ref, own_ref, x_out, send_ref):
    refs = (got1_ref, got2_ref, got3_ref)
    sent = [ref[pl.ds(FADE, 16)].astype(F32) for ref in refs]
    row = lax.broadcasted_iota(jnp.int32, (8, DIM), 0)
    fades, marks = jnp.zeros((8, DIM), F32), jnp.zeros((8, DIM), F32)
    for h in range(2):
        rows = pl.ds(h * DIM, DIM)
        f1, f2, f3 = (v[2 * h : 2 * h + 1] + v[2 * h + 1 : 2 * h + 2] for v in sent)
        g1, g2, g3 = (ref[rows].astype(F32) for ref in refs)
        before = g1 + f1 * (g2 + f2 * g3)
        x_out[rows] = before
        own = own_ref[pl.ds(FADE, 8)][h : h + 1]
        send_ref[rows] = (own * before + own_ref[rows]).astype(BF16)
        past = f1 * f2 * f3
        marks = jnp.where(row == h, past, marks)
        fade = own * past
        high = fade.astype(BF16).astype(F32)
        fades = jnp.where(row == 2 * h, high, jnp.where(row == 2 * h + 1, fade - high, fades))
    x_out[pl.ds(FADE, 8)] = marks
    send_ref[pl.ds(FADE, 16)] = jnp.concatenate([fades, jnp.zeros((8, DIM), F32)], axis=0).astype(BF16)


def local_kernel(x_ref, w_ref, r_ref, g_ref, codes_ref, rates_ref, skip_ref, base_ref, carry_ref):
    sums = code_sums(codes_ref)
    lower = lax.broadcasted_iota(jnp.int32, (BLOCK, BLOCK), 0) >= lax.broadcasted_iota(
        jnp.int32, (BLOCK, BLOCK), 1
    )
    for h in range(2):
        cols = pl.ds(h * DIM, DIM)
        rate, skip = rates_ref[h], skip_ref[h]
        state, before = None, None
        for b in range(2):
            rows = pl.ds(b * BLOCK, BLOCK)
            across, down = square(sums[b, h])
            x, w, r = x_ref[rows, cols], w_ref[rows, cols], r_ref[rows, cols]
            decay = jnp.exp(jnp.minimum(rate * (across - down), 0.0))
            scores = dot(r, w, 1, 1)
            mix = jnp.where(lower, scores * decay, 0.0).astype(BF16)
            y = dot(mix, x) + skip * x.astype(F32)
            if b == 0:
                last = down[BLOCK - 1 : BLOCK]
                tail = jnp.exp(rate * (down - last))
                state = dot((w.astype(F32) * tail).astype(BF16), x, 0, 0)
                before = last
                carry = jnp.exp(-rate * down)
            else:
                high, low = split(state)
                y = y + jnp.exp(-rate * down) * (dot(r, high) + dot(r, low))
                carry = jnp.exp(-rate * (down + before))
            gate = g_ref[rows, cols].astype(F32)
            silu = gate / (1.0 + jnp.exp(-gate))
            base_ref[rows, cols] = y * silu
            carry_ref[rows, cols] = carry * silu


def to_lanes(v):
    halves = v[:, :DIM] + v[:, DIM:]
    return [
        jnp.sum(jnp.transpose(halves[b * DIM : (b + 1) * DIM]), axis=0, keepdims=True)
        for b in range(2)
    ]


def carried_kernel(
    near_ref, mid_ref, far_ref, x_ref, r_ref, base_ref, carry_ref, rows_ref, gated_ref, stats_ref
):
    parts = []
    near, mid = near_ref[pl.ds(FADE, 16)].astype(F32), mid_ref[pl.ds(FADE, 16)].astype(F32)
    for h in range(2):
        rows, cols = pl.ds(h * DIM, DIM), pl.ds(h * DIM, DIM)
        entering = far_ref[rows].astype(F32)
        for ref, fades in ((mid_ref, mid), (near_ref, near)):
            fade = fades[2 * h : 2 * h + 1] + fades[2 * h + 1 : 2 * h + 2]
            entering = fade * entering + ref[rows].astype(F32)
        entering = x_ref[pl.ds(FADE, 8)][h : h + 1] * entering + x_ref[rows]
        high, low = split(entering)
        r = r_ref[:, cols]
        parts.append(base_ref[:, cols] + carry_ref[:, cols] * (dot(r, high) + dot(r, low)))
    gated = jnp.concatenate(parts, axis=1)
    gated_ref[...] = gated
    weight = rows_ref[1:2, :]
    stats_ref[...] = jnp.concatenate(to_lanes(gated * gated) + to_lanes(gated * weight), axis=0)


def keys_of(ref, k):
    return jnp.concatenate([ref[n, k + i, 0:64] for i in range(2) for n in range(4)], axis=0)


def values_of(ref, k):
    return jnp.concatenate([ref[n, k + i, 64:128] for i in range(2) for n in range(4)], axis=0)


def spread(q_ref, scaled_ref):
    c = math.log2(math.e) / math.sqrt(DIM)
    for h in range(2):
        high, low = split(q_ref[:, h * DIM : (h + 1) * DIM].astype(F32) * c)
        scaled_ref[pl.ds(h * 256, 256)] = jnp.concatenate([high, low], axis=1)


def scan_keys(kv_ref, core, scaled_ref, scores_ref, m_ref, l_ref, acc_ref, fresh):
    zl, here = lax.axis_index("zl"), lax.axis_index("core")
    tiles = zl + 1 if fresh else zl + here
    pairs = zl // 2 if fresh else tiles // 2
    rows = scaled_ref.shape[0]

    def lanes_max(s):
        return jnp.maximum(
            jnp.maximum(s[:, 0:128], s[:, 128:256]), jnp.maximum(s[:, 256:384], s[:, 384:512])
        )

    def scores(i):
        keys = keys_of(kv_ref, 2 * i)
        return dot(scaled_ref[...], jnp.concatenate([keys, keys], axis=1), 1, 1)

    def first(i, _):
        s = scores(i)
        scores_ref[i] = s
        m_ref[...] = jnp.maximum(m_ref[...], lanes_max(s))
        return 0

    def tail(i):
        key = lax.broadcasted_iota(jnp.int32, (rows, 512), 1)
        key = (i * 2) * 512 + core * 256 + jnp.where(key < 256, key, key + 256)
        spot = lax.broadcasted_iota(jnp.int32, (rows, 512), 0)
        spot = zl * 512 + here * 256 + jnp.where(spot < 256, spot, spot - 256)
        s = jnp.where(key <= spot, scores(i), NEG)
        scores_ref[i] = s
        m_ref[...] = jnp.maximum(m_ref[...], lanes_max(s))

    old = m_ref[...]
    lax.fori_loop(0, pairs, first, 0)
    ragged = 2 * pairs < tiles

    @pl.when(ragged)
    def _():
        tail(pairs)

    top = jnp.broadcast_to(jnp.max(m_ref[...], axis=1, keepdims=True), m_ref.shape)
    if fresh:
        l_ref[...] = jnp.zeros(l_ref.shape, F32)
        acc_ref[...] = jnp.zeros(acc_ref.shape, F32)
    else:
        fade = jnp.exp2(old - top)
        l_ref[...] = l_ref[...] * fade
        acc_ref[...] = acc_ref[...] * fade
    m_ref[...] = top

    def second(i, _):
        top = m_ref[...]
        p = [jnp.exp2(scores_ref[i, :, n : n + 128] - top) for n in range(0, 512, 128)]
        l_ref[...] += (p[0] + p[1]) + (p[2] + p[3])
        weights = jnp.concatenate([v.astype(BF16) for v in p], axis=1)
        acc_ref[...] += dot(weights, values_of(kv_ref, 2 * i))
        return 0

    lax.fori_loop(0, pairs + ragged.astype(jnp.int32), second, 0)


def attend_own_kernel(q_ref, kv_ref, scaled_ref, m_ref, l_ref, acc_ref, scores_ref):
    spread(q_ref, scaled_ref)
    m_ref[...] = jnp.full(m_ref.shape, NEG, F32)
    scan_keys(kv_ref, lax.axis_index("core"), scaled_ref, scores_ref, m_ref, l_ref, acc_ref, True)


def attend_other_kernel(
    scaled_ref, kv_ref, m_in, l_in, acc_in, rows_ref, stats_ref,
    o_ref, send_ref, m_ref, l_ref, acc_ref, scores_ref,
):
    m_ref[...] = m_in[...]
    l_ref[...] = l_in[...]
    acc_ref[...] = acc_in[...]
    other = 1 - lax.axis_index("core")
    scan_keys(kv_ref, other, scaled_ref, scores_ref, m_ref, l_ref, acc_ref, False)
    parts = []
    for h in range(2):
        at = pl.ds(h * 256, 256)
        parts.append(acc_ref[at] / jnp.sum(l_ref[at], axis=1, keepdims=True))
    attended = jnp.concatenate(parts, axis=1).astype(BF16)
    o_ref[...] = attended
    a = to_lanes(attended.astype(F32) * rows_ref[2:3, :])
    seg = [rows_ref[3:4, :DIM], rows_ref[3:4, DIM:]]
    stats = jnp.concatenate([stats_ref[...]] + a + seg, axis=0).astype(BF16)
    for n in range(send_ref.shape[0]):
        send_ref[n] = stats


def segment_row(values):
    full = jnp.concatenate([values, jnp.zeros((DIM - SEGMENTS, DIM), F32)], axis=0)
    return jnp.sum(jnp.transpose(full), axis=0, keepdims=True)


def middle_sums_kernel(got_ref, send_ref):
    segment = lax.broadcasted_iota(jnp.int32, (SEGMENTS, DIM), 0)
    plane = got_ref.shape[0] // 2
    rows = []
    for core in range(2):
        low = got_ref[core * plane].astype(F32)
        total = low
        for n in range(1, plane):
            total = total + got_ref[core * plane + n].astype(F32)
        seg = low[6:8]
        held = seg.astype(jnp.int32)
        part = jnp.zeros((SEGMENTS, DIM), F32)
        for j in range(2):
            part = part + jnp.where(held[j : j + 1] == segment, total[4 + j : 5 + j], 0.0)
        part = segment_row(part)
        high = part.astype(BF16).astype(F32)
        rows += [total[0:4], high, part - high, seg]
    out = jnp.concatenate(rows, axis=0).astype(BF16)
    for n in range(send_ref.shape[0]):
        send_ref[n] = out


def final_kernel(got_ref, gated_ref, rows_ref, o_ref, values_ref):
    zl, core = lax.axis_index("zl"), lax.axis_index("core")
    mine = got_ref[2 * zl].astype(F32) + got_ref[2 * zl + 1].astype(F32)
    mine = jnp.where(core == 0, mine[0:8], mine[8:16])
    gain = rows_ref[0:1, :]
    for b in range(2):
        rows = pl.ds(b * DIM, DIM)
        scale = lax.rsqrt(mine[b : b + 1] * (1.0 / COLUMNS) + EPS)
        _, down = square(scale)
        for h in range(2):
            cols = slice(h * DIM, (h + 1) * DIM)
            o_ref[rows, cols] = (gated_ref[rows, cols] * down * gain[:, cols]).astype(BF16)
    segment = lax.broadcasted_iota(jnp.int32, (SEGMENTS, DIM), 0)
    part = jnp.zeros((SEGMENTS, DIM), F32)
    count = jnp.zeros((SEGMENTS, DIM), F32)
    extra = jnp.zeros((8, DIM), F32)
    for s in range(got_ref.shape[0] // 2):
        low = got_ref[2 * s].astype(F32)
        pair = low + got_ref[2 * s + 1].astype(F32)
        for c in range(2):
            both = pair[8 * c : 8 * c + 8]
            extra = extra + both
            scale = lax.rsqrt(both[0:2] * (1.0 / COLUMNS) + EPS)
            score = scale * both[2:4]
            seg = low[8 * c + 6 : 8 * c + 8].astype(jnp.int32)
            for j in range(2):
                member = seg[j : j + 1] == segment
                part = part + jnp.where(member, score[j : j + 1], 0.0)
                count = count + jnp.where(member, 1.0, 0.0)
    total = segment_row(part) + extra[4:5] + extra[5:6]
    held = segment_row(count)
    values_ref[...] = (total / jnp.maximum(held, 1.0))[:, :SEGMENTS]


def per_device(
    queries,
    key_rows,
    value_rows,
    state_input,
    state_write,
    state_read,
    gate_input,
    decay_codes,
    decay_rates,
    skip_gain,
    norm_gain,
    attend_readout,
    state_readout,
    segment_index,
):
    tokens = queries.shape[0]
    codes = decay_codes.T
    seg = segment_index.reshape(1, 256)
    gain = norm_gain.reshape(1, 256)
    state_out = state_readout.reshape(1, 256)
    attend_out = attend_readout.reshape(1, 256)
    chips, wide = lax.axis_size("zl"), lax.axis_size("x")
    ctx = chips * lax.axis_size("core")

    together = lax.optimization_barrier
    packed = call(
        pack_kernel,
        shape((chips, DIM, DIM), BF16),
        [HBM] * 2,
        [pltpu.VMEM((DIM, DIM), BF16), pltpu.SemaphoreType.DMA((2,))],
        mib=PACK_MIB,
    )(key_rows, value_rows)
    packed, codes = together((packed, codes))
    quarter = lax.all_to_all(packed, "zl", 0, 0)
    own, send, rows = call(
        states_kernel,
        (shape((FADE + 8, DIM)), shape((STATE_ROWS, DIM), BF16), shape((8, 256))),
        [SMEM] + [VMEM] * 7,
    )(decay_rates, state_input, state_write, codes, gain, state_out, attend_out, seg)

    def shifted(v, by):
        return lax.ppermute(v, CTX, [(i, i + by) for i in range(ctx - by)])

    got = tuple(shifted(send, by) for by in (3, 2, 1))
    base, carry = call(
        local_kernel, (shape((tokens, 256)), shape((tokens, 256))), [VMEM] * 5 + [SMEM] * 2
    )(state_input, state_write, state_read, gate_input, codes, decay_rates, skip_gain)
    quarter, base = together((quarter, base))
    fan = call(fan_kernel, shape((wide, chips, DIM, DIM), BF16), [VMEM])(quarter)
    got, _ = together((got, fan))
    before, send = call(
        merge_kernel, (shape((FADE + 8, DIM)), shape((STATE_ROWS, DIM), BF16)), [VMEM] * 4, flops=MERGE_FLOPS
    )(*got[::-1], own)

    mine = lax.all_to_all(fan, "x", 0, 0)
    arrived = tuple(shifted(send, by) for by in (12, 4, 8))
    theirs = lax.ppermute(mine, "core", [(0, 1), (1, 0)])
    running = (shape((512, 256), BF16),) + (shape((512, DIM)),) * 3
    scores = pltpu.VMEM((chips // 2, 512, 512), F32)
    attention = call(attend_own_kernel, running, [VMEM] * 2, [scores], flops=10**9)(queries, mine)
    arrived, attention = together((arrived, attention))
    far, near, mid = arrived
    gated, stats = call(
        carried_kernel, (shape((tokens, 256)), shape((4, DIM))), [VMEM] * 8, flops=CARRIED_FLOPS
    )(near, mid, far, before, state_read, base, carry, rows)
    theirs, attention, stats = together((theirs, attention, stats))
    head_plane = lax.axis_size("y") * wide
    attended, send = call(
        attend_other_kernel,
        (shape((tokens, 256), BF16), shape((2 * head_plane, 8, DIM), BF16)),
        [VMEM] * 7,
        [pltpu.VMEM((512, DIM), F32) for _ in range(3)] + [scores],
        flops=10**9,
    )(attention[0], theirs, *attention[1:], rows, stats)
    summed = lax.all_to_all(send, ("core", "y", "x"), 0, 0)
    line = chips * lax.axis_size("zh")
    send = call(middle_sums_kernel, shape((line, 16, DIM), BF16), [VMEM])(summed)
    summed = lax.all_to_all(send, ("zl", "zh"), 0, 0)
    state_mixed, values = call(
        final_kernel, (shape((tokens, 256), BF16), shape((1, SEGMENTS))), [VMEM] * 3
    )(summed, gated, rows)
    return attended, state_mixed, values.reshape(SEGMENTS)


def solution(mesh):
    grid = mesh.devices.shape
    inner = Mesh(mesh.devices.reshape(grid[0] // 2, 2, 2, 4, grid[1] // 8), CTX + HEAD)
    both = P(CTX, HEAD)
    rows, heads = P(CTX), P(HEAD)
    in_specs = (both, P(CTX, None), P(CTX, None)) + (both,) * 5 + (heads,) * 5 + (rows,)
    return jax.shard_map(
        per_device, mesh=inner, in_specs=in_specs, out_specs=(both, both, P()), check_vma=False
    )
```
